128 devices in a mesh: lon: 16 (over z, x_lo, core), ens: 8 (over y, x_hi).
Axes of the slice: x: 4 (x_hi: 2, x_lo: 2; x = x_hi * 2 + x_lo), y: 4, z: 4, core: 2. Of those that a mesh axis runs over, the one named last changes fastest.
Arguments:
- features: bfloat16 [16, 4, 1440, 512], P('ens', None, 'lon'), may hold values from -6 to 6
- weight: bfloat16 [2048, 512], P('ens'), may hold values from -0.125 to 0.125
- grad_out: bfloat16 [16, 4, 1440, 512], P('ens', None, 'lon'), may hold values from -6 to 6
- band_width: int32 [4], replicated, may hold values from 4 to 1440, as said below
- band_start: int32 [4], replicated, may hold values from -722 to 0, as said below
Outputs:
- output: bfloat16 [16, 4, 1440, 512], P('ens', None, 'lon')
- grad_input: bfloat16 [16, 4, 1440, 512], P('ens', None, 'lon')
- grad_weight: float32 [2048, 512], P('ens')
The draws below stay inside these ranges and needn't reach their ends.
Inputs may be any that keep to these rules, and one draw needn't show every extreme that they name: band_width[0] equals 1440, so the first row's support covers the whole circle; the last row's width is 4. The support of row l is the band_width[l] consecutive longitudes starting band_start[l] cells from the target, taken cyclically; the first row starts at -720 - 2 and the last row at 0.
All inputs are finite; a program needn't handle non-finite values.
Results may differ from the reference program's by a relative error of at most 0.0055.
Values may be sent and summed in bfloat16 or wider, within the bound.
A program may use at most 128 MiB of HBM per device.

```python
import jax
import jax.numpy as jnp

C = 512
K = 4
LAT = 4
NLON = 1440
E = 16


def band_common(key):
    widths = jax.random.randint(key, (LAT,), 4, NLON + 1, dtype=jnp.int32)
    rows = jnp.arange(LAT)
    widths = jnp.where(rows == LAT - 1, 4, widths)
    return jnp.where(rows == 0, NLON, widths).astype(jnp.int32)


def draw_band_width(key, part):
    widths = band_common(key)
    return widths


def draw_band_start(key, part):
    widths = band_common(key)
    key = jax.random.fold_in(key, 2)
    shifts = jax.random.randint(key, (LAT,), -2, 3, dtype=jnp.int32)
    rows = jnp.arange(LAT)
    starts = shifts - widths // 2
    starts = jnp.where(rows == 0, -(NLON // 2) - 2, starts)
    starts = jnp.where(rows == LAT - 1, 0, starts)
    return starts.astype(jnp.int32)


def level_of(key, dims, shards, low, largest):
    gain = 1.0
    for dim, shards_of in shards:
        draws = jax.random.uniform(jax.random.fold_in(jax.random.fold_in(key, 6), dim), (shards_of,), jnp.float32, low / len(shards), largest / len(shards))
        gain = gain * jnp.repeat(jnp.exp(draws), dims[dim] // shards_of).reshape((-1,) + (1,) * (len(dims) - 1 - dim))
    return gain


def scatter_about(stream_key, extent, deviation, most, pieces=(), kind=jnp.bfloat16):
    result = deviation * jax.random.normal(stream_key, extent, jnp.float32)
    if pieces:
        result = result * level_of(stream_key, extent, pieces, -0.22, 0.18)
    return jnp.clip(result, -most, most).astype(kind)


def setup_inputs(seed: int = 0) -> dict:
    splits = jax.random.split(jax.random.key(seed), 6)
    features = scatter_about(splits[0], (E, LAT, NLON, C), 1.0, 6.0, ((0, 8), (2, 16)))
    weight = scatter_about(splits[1], (K * C, C), (K * C) ** -0.5, 0.125, ((0, 8),))
    grad_out = scatter_about(splits[2], (E, LAT, NLON, C), 1.0, 6.0, ((0, 8), (2, 16)))
    band_width = draw_band_width(jax.random.fold_in(splits[5], 71), 0)
    band_start = draw_band_start(jax.random.fold_in(splits[5], 71), 0)
    return {"features": features, "weight": weight, "grad_out": grad_out, "band_width": band_width, "band_start": band_start}


def make_basis(widths, starts, targets, sources):
    relative = jnp.mod(sources[None, None, :] - targets[None, :, None] - starts[:, None, None], NLON)
    inside = relative < widths[:, None, None]
    width_float = widths.astype(jnp.float32)[:, None, None]
    position = (relative.astype(jnp.float32) + 0.5) * (K - 1) / width_float
    orders = jnp.arange(K).astype(jnp.float32)
    hats = jnp.maximum(0.0, 1.0 - jnp.abs(position[:, None] - orders[None, :, None, None]))
    hats = hats / jnp.sqrt(width_float)[:, None]
    return jnp.where(inside[:, None], hats, 0.0).astype(jnp.bfloat16)

def reference(features, weight, grad_out, band_width, band_start):
    longitudes = jnp.arange(NLON).astype(jnp.int32)
    responses = []
    adjoints = []
    for row in range(LAT):
        kernel = make_basis(band_width[row:row + 1], band_start[row:row + 1], longitudes, longitudes)[0].astype(jnp.float32)
        responses.append(jnp.einsum('kts,msc->mtkc', kernel, features[:, row].astype(jnp.float32)).astype(jnp.bfloat16))
        adjoints.append(jnp.einsum('kts,mtd->mskd', kernel, grad_out[:, row].astype(jnp.float32)).astype(jnp.bfloat16))
    response = jnp.stack(responses, axis=1).reshape(E * LAT * NLON, K * C)
    adjoint = jnp.stack(adjoints, axis=1).reshape(E * LAT * NLON, K, C)
    output = jnp.dot(response, weight, preferred_element_type=jnp.float32).astype(jnp.bfloat16)
    grad_input = jnp.einsum('rkd,kcd->rc', adjoint.astype(jnp.float32), weight.reshape(K, C, C).astype(jnp.float32)).astype(jnp.bfloat16)
    grad_weight = jnp.dot(response.T, grad_out.reshape(E * LAT * NLON, C), preferred_element_type=jnp.float32)
    return (output.reshape(E, LAT, NLON, C), grad_input.reshape(E, LAT, NLON, C), grad_weight)
```

```python
import functools

import jax
import jax.numpy as jnp
from jax import lax
from jax.experimental import pallas as pl
from jax.experimental.pallas import tpu as pltpu
from jax.sharding import PartitionSpec as P

K = 4
BF = jnp.bfloat16
F32 = jnp.float32


def remote(src, dst, send, recv, lon, ens):
    return pltpu.make_async_remote_copy(
        src_ref=src,
        dst_ref=dst,
        send_sem=send,
        recv_sem=recv,
        device_id={"lon": lon, "ens": ens},
        device_id_type=pl.DeviceIdType.MESH,
    )


def fill_strip(strip, width, start, block, padded, count, flip):
    circle = block * count
    step = min(128, padded * count)
    row = lax.broadcasted_iota(jnp.int32, (padded, step), 0)
    lane = lax.broadcasted_iota(jnp.int32, (padded, step), 1)
    wide = jnp.full((1, step), width.astype(F32), F32)
    scale = 1.0 / jnp.sqrt(wide)
    for first in range(0, padded * count, step):
        column = lane + first
        low = first // padded
        part = jnp.full_like(column, low)
        for edge in range(low + 1, (first + step - 1) // padded + 1):
            part = part + (column >= edge * padded).astype(jnp.int32)
        inner = column - part * padded
        place = inner + part * block
        valid = (inner < block) & (row < block)
        away = (row - place if flip else place - row) - start
        away = jnp.where(away < 0, away + circle, away)
        away = jnp.where(away >= circle, away - circle, away)
        inside = valid & (away < width)
        position = (away.astype(F32) + 0.5) * (K - 1) / wide
        for k in range(K):
            hat = jnp.maximum(0.0, 1.0 - jnp.abs(position - float(k))) * scale
            strip[pl.ds(k * padded, padded), pl.ds(first, step)] = jnp.where(inside, hat, 0.0).astype(BF)


def kernel(
    count, groups,
    f_ref, g_ref, w_ref, width_ref, start_ref,
    out_ref, gi_ref, gw_ref,
    f_send, g_send, f_ext, g_ext, f_strip, g_strip, resp, adj, w_all,
    out_own, gi_own, out_in, gi_in,
    gw_own, gw_half, gw_mate, gw_sum, gw_ens, gw_lon, gw_lon_in, gw_full,
    f_ss, f_rs, f_fs, g_ss, g_rs, g_fs, w_ss, w_rs, w_ms, w_mr,
    out_ss, out_rs, gi_ss, gi_rs,
    a_ss, a_rs, b_ss, b_rs, c_ss, c_rs, d_ss, d_rs,
):
    members, rows, block, channels = f_ref.shape
    padded = f_send.shape[1]
    tasks = members * rows
    lon = lax.axis_index("lon")
    ens = lax.axis_index("ens")
    half = lax.rem(lon, 2)
    task = lax.div(lon, 2)
    mate = lon + 1 - 2 * half

    barrier = pltpu.get_barrier_semaphore()

    @pl.loop(1, count)
    def _(o):
        pl.semaphore_signal(barrier, inc=1, device_id={"lon": lax.rem(lon + o, count), "ens": ens},
                            device_id_type=pl.DeviceIdType.MESH)

    @pl.loop(1, groups)
    def _(o):
        pl.semaphore_signal(barrier, inc=1, device_id={"lon": lon, "ens": lax.rem(ens + o, groups)},
                            device_id_type=pl.DeviceIdType.MESH)

    def stage(ref, buffer, ext):
        for q in range(tasks):
            buffer[q, pl.ds(padded - 16, 16), :] = jnp.zeros((16, channels), BF)
            buffer[q, pl.ds(0, block), :] = ref[q // rows, q % rows]
        ext[lon] = buffer[task]

    piece = w_ref.shape[0] // 2
    w_all[ens, 0] = w_ref[0:piece]
    w_all[ens, 1] = w_ref[piece:]
    stage(g_ref, g_send, g_ext)
    stage(f_ref, f_send, f_ext)

    pl.semaphore_wait(barrier, count - 1 + groups - 1)

    def w_copy(o):
        return remote(w_all.at[ens, half], w_all.at[ens, half], w_ss.at[o], w_rs.at[ens],
                      lon, lax.rem(ens + o, groups))

    def w_from(o):
        other = lax.rem(ens + groups - o, groups)
        return remote(w_all.at[other, half], w_all.at[other, half], w_ss.at[o], w_rs.at[other], lon, other)

    def in_copy(buffer, ext, ss, rs, o):
        q = lax.rem(task + o, tasks)
        return remote(buffer.at[q], ext.at[lon], ss.at[o], rs.at[lon], 2 * q + half, ens)

    def in_from(ext, ss, rs, o):
        slot = 2 * lax.rem(task + tasks - o, tasks) + half
        return remote(ext.at[slot], ext.at[slot], ss.at[o], rs.at[slot], slot, ens)

    def forward(ext, fs, rs, o):
        slot = 2 * lax.rem(task + tasks - o, tasks) + half
        return remote(ext.at[slot], ext.at[slot], fs.at[o], rs.at[slot], mate, ens)

    def forwarded(ext, fs, rs, o):
        slot = 2 * lax.rem(task + tasks - o, tasks) + 1 - half
        return remote(ext.at[slot], ext.at[slot], fs.at[o], rs.at[slot], mate, ens)

    @pl.loop(1, groups)
    def _(o):
        w_copy(o).start()

    @pl.loop(1, tasks)
    def _(o):
        in_copy(g_send, g_ext, g_ss, g_rs, o).start()

    @pl.loop(1, tasks)
    def _(o):
        in_copy(f_send, f_ext, f_ss, f_rs, o).start()

    forward(g_ext, g_fs, g_rs, 0).start()
    forward(f_ext, f_fs, f_rs, 0).start()

    row = lax.rem(task, rows)
    fill_strip(g_strip, width_ref[row], start_ref[row], block, padded, count, True)
    fill_strip(f_strip, width_ref[row], start_ref[row], block, padded, count, False)

    def arrive(ext, ss, fs, rs):
        @pl.loop(1, tasks)
        def _(o):
            in_from(ext, ss, rs, o).wait_recv()
            forward(ext, fs, rs, o).start()

        @pl.loop(0, tasks)
        def _(o):
            forwarded(ext, fs, rs, o).wait_recv()

        @pl.loop(0, count - 1)
        def _(b):
            ext[count + b] = ext[b]

    def convolve(strip, ext, result):
        @pl.loop(0, tasks)
        def _(n):
            window = ext[pl.ds(2 * n + half, count)].reshape(count * padded, channels)
            total = jnp.dot(strip[...], window, preferred_element_type=F32)
            for k in range(K):
                result[k, n] = total[k * padded:(k + 1) * padded].astype(BF)

    per = groups // K

    def weight_of(k):
        return w_all[pl.ds(k * per, per)].reshape(channels, channels)

    def back_copy(own, into, ss, rs, n):
        return remote(own.at[n], into.at[task], ss.at[n], rs.at[task], 2 * n + half, ens)

    def back_from(own, into, ss, rs, n):
        return remote(own.at[n], into.at[n], ss.at[n], rs.at[n], 2 * n + half, ens)

    def mix(source, own, into, ss, rs, flip):
        chunk = tasks // 2
        for c in range(2):
            total = None
            for k in range(K):
                part = source[k, pl.ds(c * chunk, chunk)].reshape(chunk * padded, channels)
                dims = (((1,), (1 if flip else 0,)), ((), ()))
                term = lax.dot_general(part, weight_of(k), dims, preferred_element_type=F32)
                total = term if total is None else total + term
            own[pl.ds(c * chunk, chunk)] = total.astype(BF).reshape(chunk, padded, channels)
            for n in range(c * chunk, (c + 1) * chunk):
                @pl.when(n != task)
                def _():
                    back_copy(own, into, ss, rs, n).start()

    arrive(g_ext, g_ss, g_fs, g_rs)

    @pl.loop(1, groups)
    def _(o):
        w_from(o).wait_recv()

    w_mate = remote(w_all.at[:, half], w_all.at[:, half], w_ms, w_mr, mate, ens)
    w_mate.start()
    convolve(g_strip, g_ext, adj)
    remote(w_all.at[:, 1 - half], w_all.at[:, 1 - half], w_ms, w_mr, mate, ens).wait_recv()
    mix(adj, gi_own, gi_in, gi_ss, gi_rs, True)

    arrive(f_ext, f_ss, f_fs, f_rs)
    own_rows = jnp.concatenate([f_ext[2 * n + half] for n in range(tasks)], axis=0)
    turned = own_rows.T
    for k in range(K):
        term = jnp.dot(turned, adj[k].reshape(tasks * padded, channels), preferred_element_type=F32)
        gw_own[pl.ds(k * per, per)] = term.reshape(per, 2, piece, channels)
    gw_half[...] = gw_own[:, 1 - half].astype(BF)
    a_copy = remote(gw_half, gw_mate, a_ss, a_rs, mate, ens)
    a_copy.start()

    convolve(f_strip, f_ext, resp)

    a_copy.wait_recv()
    gw_sum[...] = (gw_own[:, half] + gw_mate[...].astype(F32)).astype(BF)

    def b_copy(o):
        other = lax.rem(ens + o, groups)
        return remote(gw_sum.at[other], gw_ens.at[ens], b_ss.at[o], b_rs.at[ens], lon, other)

    def b_from(o):
        other = lax.rem(ens + groups - o, groups)
        return remote(gw_sum.at[other], gw_ens.at[other], b_ss.at[o], b_rs.at[other], lon, other)

    @pl.loop(1, groups)
    def _(o):
        b_copy(o).start()

    gw_ens[ens] = gw_sum[ens]
    mix(resp, out_own, out_in, out_ss, out_rs, False)

    @pl.loop(1, groups)
    def _(o):
        b_from(o).wait_recv()

    total = gw_ens[0].astype(F32)
    for e in range(1, groups):
        total = total + gw_ens[e].astype(F32)
    gw_lon[...] = total.astype(BF).reshape(gw_lon.shape)

    def c_copy(o):
        q = lax.rem(task + o, tasks)
        return remote(gw_lon.at[q], gw_lon_in.at[task], c_ss.at[o], c_rs.at[task], 2 * q + half, ens)

    def c_from(o):
        q = lax.rem(task + tasks - o, tasks)
        return remote(gw_lon.at[q], gw_lon_in.at[q], c_ss.at[o], c_rs.at[q], 2 * q + half, ens)

    @pl.loop(1, tasks)
    def _(o):
        c_copy(o).start()

    gw_lon_in[task] = gw_lon[task]

    @pl.loop(1, tasks)
    def _(o):
        c_from(o).wait_recv()

    total = gw_lon_in[0].astype(F32)
    for q in range(1, tasks):
        total = total + gw_lon_in[q].astype(F32)
    gw_full[lon] = total

    def d_copy(o):
        return remote(gw_full.at[lon], gw_full.at[lon], d_ss.at[o], d_rs.at[lon], lax.rem(lon + o, count), ens)

    def d_from(o):
        other = lax.rem(lon + count - o, count)
        return remote(gw_full.at[other], gw_full.at[other], d_ss.at[o], d_rs.at[other], other, ens)

    @pl.loop(1, count)
    def _(o):
        d_copy(o).start()

    def finish(ref, own, into, ss, rs):
        into[task] = own[task]
        for q in range(tasks):
            @pl.when(q != task)
            def _():
                back_from(own, into, ss, rs, q).wait_recv()
            ref[q // rows, q % rows] = into[q, pl.ds(0, block), :]

    finish(gi_ref, gi_own, gi_in, gi_ss, gi_rs)
    finish(out_ref, out_own, out_in, out_ss, out_rs)

    @pl.loop(1, count)
    def _(o):
        d_from(o).wait_recv()

    strip_rows = gw_full.shape[1]
    for q in range(tasks):
        for s in range(2):
            gw_ref[pl.ds(s * piece + q * strip_rows, strip_rows), :] = gw_full[2 * q + s]

    @pl.loop(1, groups)
    def _(o):
        w_copy(o).wait_send()
        b_copy(o).wait_send()

    w_mate.wait_send()
    a_copy.wait_send()

    @pl.loop(0, tasks)
    def _(o):
        forward(g_ext, g_fs, g_rs, o).wait_send()
        forward(f_ext, f_fs, f_rs, o).wait_send()

    @pl.loop(1, tasks)
    def _(o):
        in_copy(g_send, g_ext, g_ss, g_rs, o).wait_send()
        in_copy(f_send, f_ext, f_ss, f_rs, o).wait_send()
        c_copy(o).wait_send()

    @pl.loop(1, count)
    def _(o):
        d_copy(o).wait_send()

    for n in range(tasks):
        @pl.when(n != task)
        def _():
            back_copy(gi_own, gi_in, gi_ss, gi_rs, n).wait_send()
            back_copy(out_own, out_in, out_ss, out_rs, n).wait_send()


def on_device(features, weight, grad_out, band_width, band_start):
    members, rows, block, channels = features.shape
    count = lax.axis_size("lon")
    groups = lax.axis_size("ens")
    tasks = members * rows
    padded = -(-block // 16) * 16
    shard = weight.shape[0]
    piece = shard // 2
    strip_rows = piece // tasks
    vmem = pltpu.VMEM
    dma = pltpu.SemaphoreType.DMA
    field = vmem((tasks, padded, channels), BF)
    ext = vmem((2 * count, padded, channels), BF)
    strip = vmem((K * padded, count * padded), BF)
    wide = vmem((K, tasks, padded, channels), BF)
    scratch = [
        field, field, ext, ext, strip, strip, wide, wide,
        vmem((groups, 2, piece, channels), BF),
        field, field, field, field,
        vmem((groups, 2, piece, channels), F32),
        vmem((groups, piece, channels), BF),
        vmem((groups, piece, channels), BF),
        vmem((groups, piece, channels), BF),
        vmem((groups, piece, channels), BF),
        vmem((tasks, strip_rows, channels), BF),
        vmem((tasks, strip_rows, channels), BF),
        vmem((count, strip_rows, channels), F32),
        dma((tasks,)), dma((count,)), dma((tasks,)),
        dma((tasks,)), dma((count,)), dma((tasks,)),
        dma((groups,)), dma((groups,)), dma(()), dma(()),
        dma((tasks,)), dma((tasks,)), dma((tasks,)), dma((tasks,)),
        dma(()), dma(()), dma((groups,)), dma((groups,)),
        dma((tasks,)), dma((tasks,)), dma((count,)), dma((count,)),
    ]
    whole = pl.BlockSpec(memory_space=pltpu.VMEM)
    scalar = pl.BlockSpec(memory_space=pltpu.SMEM)
    return pl.pallas_call(
        functools.partial(kernel, count, groups),
        out_shape=(
            jax.ShapeDtypeStruct(features.shape, BF),
            jax.ShapeDtypeStruct(features.shape, BF),
            jax.ShapeDtypeStruct(weight.shape, F32),
        ),
        in_specs=[whole, whole, whole, scalar, scalar],
        out_specs=(whole, whole, whole),
        scratch_shapes=scratch,
        compiler_params=pltpu.CompilerParams(
            collective_id=0, has_side_effects=True, vmem_limit_bytes=60 * 1024 * 1024
        ),
    )(features, grad_out, weight, band_width, band_start)


def solution(mesh):
    placed = (P("ens", None, "lon", None), P("ens", None), P("ens", None, "lon", None), P(), P())
    return jax.shard_map(
        on_device,
        mesh=mesh,
        in_specs=placed,
        out_specs=(P("ens", None, "lon", None), P("ens", None, "lon", None), P("ens", None)),
        check_vma=False,
    )
```

```python
import functools

import jax
import jax.numpy as jnp
from jax import lax
from jax.experimental import pallas as pl
from jax.experimental.pallas import tpu as pltpu
from jax.sharding import PartitionSpec as P

K = 4
BF = jnp.bfloat16
F32 = jnp.float32


def remote(src, dst, send, recv, lon, ens):
    return pltpu.make_async_remote_copy(
        src_ref=src,
        dst_ref=dst,
        send_sem=send,
        recv_sem=recv,
        device_id={"lon": lon, "ens": ens},
        device_id_type=pl.DeviceIdType.MESH,
    )


def fill_strip(strip, width, start, block, padded, count, flip):
    circle = block * count
    step = min(128, padded * count)
    row = lax.broadcasted_iota(jnp.int32, (padded, step), 0)
    lane = lax.broadcasted_iota(jnp.int32, (padded, step), 1)
    wide = jnp.full((1, step), width.astype(F32), F32)
    scale = 1.0 / jnp.sqrt(wide)
    for first in range(0, padded * count, step):
        column = lane + first
        low = first // padded
        part = jnp.full_like(column, low)
        for edge in range(low + 1, (first + step - 1) // padded + 1):
            part = part + (column >= edge * padded).astype(jnp.int32)
        inner = column - part * padded
        place = inner + part * block
        valid = (inner < block) & (row < block)
        away = (row - place if flip else place - row) - start
        away = jnp.where(away < 0, away + circle, away)
        away = jnp.where(away >= circle, away - circle, away)
        inside = valid & (away < width)
        position = (away.astype(F32) + 0.5) * (K - 1) / wide
        for k in range(K):
            hat = jnp.maximum(0.0, 1.0 - jnp.abs(position - float(k))) * scale
            strip[pl.ds(k * padded, padded), pl.ds(first, step)] = jnp.where(inside, hat, 0.0).astype(BF)


def spread(block, padded, rows):
    to = lax.broadcasted_iota(jnp.int32, (rows * padded, block * rows), 0)
    source = lax.broadcasted_iota(jnp.int32, (rows * padded, block * rows), 1)
    row = sum((to >= padded * r).astype(jnp.int32) for r in range(1, rows))
    place = to - padded * row
    return ((source == place * rows + row) & (place < block)).astype(F32).astype(BF)


def gather_back(block, padded, rows):
    to = lax.broadcasted_iota(jnp.int32, (block * rows, rows * padded), 0)
    source = lax.broadcasted_iota(jnp.int32, (block * rows, rows * padded), 1)
    place = lax.div(to, rows)
    return (source == (to - place * rows) * padded + place).astype(F32).astype(BF)


def kernel(
    count, groups,
    f_ref, g_ref, w_ref, width_ref, start_ref,
    out_ref, gi_ref, gw_ref,
    f_send, g_send, f_ext, g_ext, f_strip, g_strip, resp, adj, w_all,
    out_own, gi_own, out_in, gi_in,
    gw_own, gw_half, gw_mate, gw_sum, gw_line, gw_part, gw_part_in, gw_full,
    f_ss, f_rs, f_fs, g_ss, g_rs, g_fs, w_ss, w_rs, w_ms, w_mr,
    out_ss, out_rs, gi_ss, gi_rs,
    a_ss, a_rs, b_ss, b_rs, c_ss, c_rs, d_ss, d_rs,
):
    members, block, rows, channels = f_ref.shape
    padded = f_send.shape[1]
    tasks = members * rows
    lon = lax.axis_index("lon")
    ens = lax.axis_index("ens")
    half = lax.rem(lon, 2)
    task = lax.div(lon, 2)
    mate = lon + 1 - 2 * half
    side = lax.rem(ens, 2)
    line = lax.div(ens, 2)
    lines = groups // 2
    across = ens + 1 - 2 * side

    barrier = pltpu.get_barrier_semaphore()

    @pl.loop(1, count)
    def _(o):
        pl.semaphore_signal(barrier, inc=1, device_id={"lon": lax.rem(lon + o, count), "ens": ens},
                            device_id_type=pl.DeviceIdType.MESH)

    @pl.loop(1, lines)
    def _(o):
        pl.semaphore_signal(barrier, inc=1, device_id={"lon": lon, "ens": 2 * lax.rem(line + o, lines) + side},
                            device_id_type=pl.DeviceIdType.MESH)

    @pl.loop(0, tasks)
    def _(q):
        pl.semaphore_signal(barrier, inc=1, device_id={"lon": 2 * q + half, "ens": across},
                            device_id_type=pl.DeviceIdType.MESH)

    def stage(ref, buffer, ext):
        for m in range(members):
            flat = ref[m].reshape(block * rows, channels)
            moved = jnp.dot(to_rows, flat, preferred_element_type=F32).astype(BF)
            buffer[pl.ds(m * rows, rows)] = moved.reshape(rows, padded, channels)
        ext[lon] = buffer[task]

    piece = w_ref.shape[0] // 2
    w_all[ens, 0] = w_ref[0:piece]
    w_all[ens, 1] = w_ref[piece:]
    to_rows = spread(block, padded, rows)
    stage(g_ref, g_send, g_ext)
    stage(f_ref, f_send, f_ext)

    pl.semaphore_wait(barrier, count - 1 + lines - 1 + tasks)

    w_across = remote(w_all.at[ens, half], w_all.at[ens, half], w_ss.at[0], w_rs.at[ens], lon, across)

    def along(o):
        return 2 * lax.rem(line + o, lines) + side

    def w_copy(o):
        return remote(w_all.at[ens, half], w_all.at[ens, half], w_ss.at[o], w_rs.at[ens], lon, along(o))

    def w_second(o):
        return remote(w_all.at[across, half], w_all.at[across, half], w_ss.at[lines + o], w_rs.at[across], lon, along(o))

    def w_from(o):
        other = lax.rem(ens + groups - o, groups)
        return remote(w_all.at[other, half], w_all.at[other, half], w_ss.at[0], w_rs.at[other], lon, other)

    def in_copy(buffer, ext, ss, rs, o):
        q = lax.rem(task + o, tasks)
        return remote(buffer.at[q], ext.at[lon], ss.at[o], rs.at[lon], 2 * q + half, ens)

    def in_from(ext, ss, rs, o):
        slot = 2 * lax.rem(task + tasks - o, tasks) + half
        return remote(ext.at[slot], ext.at[slot], ss.at[o], rs.at[slot], slot, ens)

    def forward(ext, fs, rs, o):
        slot = 2 * lax.rem(task + tasks - o, tasks) + half
        return remote(ext.at[slot], ext.at[slot], fs.at[o], rs.at[slot], mate, ens)

    def forwarded(ext, fs, rs, o):
        slot = 2 * lax.rem(task + tasks - o, tasks) + 1 - half
        return remote(ext.at[slot], ext.at[slot], fs.at[o], rs.at[slot], mate, ens)

    w_across.start()

    @pl.loop(1, lines)
    def _(o):
        w_copy(o).start()

    @pl.loop(1, tasks)
    def _(o):
        in_copy(g_send, g_ext, g_ss, g_rs, o).start()

    @pl.loop(1, tasks)
    def _(o):
        in_copy(f_send, f_ext, f_ss, f_rs, o).start()

    forward(g_ext, g_fs, g_rs, 0).start()
    forward(f_ext, f_fs, f_rs, 0).start()

    remote(w_all.at[across, half], w_all.at[across, half], w_ss.at[0], w_rs.at[across], lon, across).wait_recv()

    @pl.loop(1, lines)
    def _(o):
        w_second(o).start()

    row = lax.rem(task, rows)
    fill_strip(g_strip, width_ref[row], start_ref[row], block, padded, count, True)
    fill_strip(f_strip, width_ref[row], start_ref[row], block, padded, count, False)

    def arrive(ext, ss, fs, rs):
        @pl.loop(1, tasks)
        def _(o):
            in_from(ext, ss, rs, o).wait_recv()
            forward(ext, fs, rs, o).start()

        @pl.loop(0, tasks)
        def _(o):
            forwarded(ext, fs, rs, o).wait_recv()

        @pl.loop(0, count - 1)
        def _(b):
            ext[count + b] = ext[b]

    def convolve(strip, ext, result):
        @pl.loop(0, tasks)
        def _(n):
            window = ext[pl.ds(2 * n + half, count)].reshape(count * padded, channels)
            total = jnp.dot(strip[...], window, preferred_element_type=F32)
            for k in range(K):
                result[k, n] = total[k * padded:(k + 1) * padded].astype(BF)

    def weight_of(k):
        return w_all[pl.ds(2 * k, 2)].reshape(channels, channels)

    def back_copy(own, into, ss, rs, n):
        return remote(own.at[n], into.at[task], ss.at[n], rs.at[task], 2 * n + half, ens)

    def back_from(own, into, ss, rs, n):
        return remote(own.at[n], into.at[n], ss.at[n], rs.at[n], 2 * n + half, ens)

    def mix(source, own, into, ss, rs, flip):
        chunk = tasks // 2
        for c in range(2):
            total = None
            for k in range(K):
                part = source[k, pl.ds(c * chunk, chunk)].reshape(chunk * padded, channels)
                dims = (((1,), (1 if flip else 0,)), ((), ()))
                term = lax.dot_general(part, weight_of(k), dims, preferred_element_type=F32)
                total = term if total is None else total + term
            own[pl.ds(c * chunk, chunk)] = total.astype(BF).reshape(chunk, padded, channels)
            for n in range(c * chunk, (c + 1) * chunk):
                @pl.when(n != task)
                def _():
                    back_copy(own, into, ss, rs, n).start()

    arrive(g_ext, g_ss, g_fs, g_rs)

    @pl.loop(1, groups)
    def _(o):
        @pl.when(lax.rem(ens + groups - o, groups) != across)
        def _():
            w_from(o).wait_recv()

    w_mate = remote(w_all.at[:, half], w_all.at[:, half], w_ms, w_mr, mate, ens)
    w_mate.start()
    convolve(g_strip, g_ext, adj)
    remote(w_all.at[:, 1 - half], w_all.at[:, 1 - half], w_ms, w_mr, mate, ens).wait_recv()
    mix(adj, gi_own, gi_in, gi_ss, gi_rs, True)

    arrive(f_ext, f_ss, f_fs, f_rs)
    own_rows = jnp.concatenate([f_ext[2 * n + half] for n in range(tasks)], axis=0)
    turned = own_rows.T

    def a_copy(o):
        to = lax.rem(line + o, lines)
        return remote(gw_half.at[to], gw_mate.at[to], a_ss.at[o], a_rs.at[to], mate, ens)

    def a_from(o):
        to = lax.rem(line + o, lines)
        return remote(gw_half.at[to], gw_mate.at[to], a_ss.at[o], a_rs.at[to], mate, ens)

    @pl.loop(1, lines + 1)
    def _(o):
        to = lax.rem(line + o, lines)
        term = jnp.dot(turned, adj[to].reshape(tasks * padded, channels), preferred_element_type=F32)
        gw_own[to] = term.reshape(2, 2, piece, channels)
        gw_half[to] = gw_own[to, :, 1 - half].astype(BF)
        a_copy(o).start()

    def b_copy(o):
        to = lax.rem(line + o, lines)
        return remote(gw_sum.at[to], gw_line.at[line], b_ss.at[o], b_rs.at[line], lon, along(o))

    def b_from(o):
        other = lax.rem(line + lines - o, lines)
        return remote(gw_sum.at[other], gw_line.at[other], b_ss.at[o], b_rs.at[other], lon, 2 * other + side)

    @pl.loop(1, lines)
    def _(o):
        to = lax.rem(line + o, lines)
        a_from(o).wait_recv()
        gw_sum[to] = (gw_own[to, :, half] + gw_mate[to].astype(F32)).astype(BF)
        b_copy(o).start()

    a_from(lines).wait_recv()

    convolve(f_strip, f_ext, resp)
    mix(resp, out_own, out_in, out_ss, out_rs, False)

    total = gw_own[line, :, half] + gw_mate[line].astype(F32)
    for o in range(1, lines):
        b_from(o).wait_recv()
        total = total + gw_line[lax.rem(line + lines - o, lines)].astype(F32)
    gw_part[...] = total.astype(BF).reshape(gw_part.shape)

    def c_place(o):
        s = lax.rem(side + lax.div(o, tasks), 2)
        return s, lax.rem(task + lax.rem(o, tasks), tasks)

    def c_copy(o):
        s, q = c_place(o)
        return remote(gw_part.at[s, q], gw_part_in.at[side, task], c_ss.at[o], c_rs.at[side, task], 2 * q + half, 2 * line + s)

    def c_from(o):
        s, q = c_place(o)
        return remote(gw_part.at[s, q], gw_part_in.at[s, q], c_ss.at[o], c_rs.at[s, q], 2 * q + half, 2 * line + s)

    @pl.loop(1, 2 * tasks)
    def _(o):
        c_copy(o).start()

    gw_part_in[side, task] = gw_part[side, task]

    def d_copy(o):
        return remote(gw_full.at[lon], gw_full.at[lon], d_ss.at[o], d_rs.at[lon], lax.rem(lon + o, count), ens)

    def d_from(o):
        other = lax.rem(lon + count - o, count)
        return remote(gw_full.at[other], gw_full.at[other], d_ss.at[o], d_rs.at[other], other, ens)

    def finish(ref, own, into, ss, rs):
        into[task] = own[task]
        for m in range(members):
            for q in range(m * rows, (m + 1) * rows):
                @pl.when(q != task)
                def _():
                    back_from(own, into, ss, rs, q).wait_recv()
            flat = into[pl.ds(m * rows, rows)].reshape(rows * padded, channels)
            moved = jnp.dot(to_places, flat, preferred_element_type=F32).astype(BF)
            ref[m] = moved.reshape(block, rows, channels)

    to_places = gather_back(block, padded, rows)
    finish(gi_ref, gi_own, gi_in, gi_ss, gi_rs)

    @pl.loop(1, 2 * tasks)
    def _(o):
        c_from(o).wait_recv()

    total = None
    for e in range(2):
        for q in range(tasks):
            term = gw_part_in[e, q].astype(F32)
            total = term if total is None else total + term
    gw_full[lon] = total.astype(BF)

    @pl.loop(1, count)
    def _(o):
        d_copy(o).start()

    finish(out_ref, out_own, out_in, out_ss, out_rs)

    @pl.loop(1, count)
    def _(o):
        d_from(o).wait_recv()

    strip_rows = gw_full.shape[1]
    for q in range(tasks):
        for s in range(2):
            gw_ref[pl.ds(s * piece + q * strip_rows, strip_rows), :] = gw_full[2 * q + s].astype(F32)

    w_across.wait_send()
    w_mate.wait_send()

    @pl.loop(1, lines)
    def _(o):
        w_copy(o).wait_send()
        w_second(o).wait_send()
        b_copy(o).wait_send()

    @pl.loop(1, lines + 1)
    def _(o):
        a_copy(o).wait_send()

    @pl.loop(1, 2 * tasks)
    def _(o):
        c_copy(o).wait_send()

    @pl.loop(0, tasks)
    def _(o):
        forward(g_ext, g_fs, g_rs, o).wait_send()
        forward(f_ext, f_fs, f_rs, o).wait_send()

    @pl.loop(1, tasks)
    def _(o):
        in_copy(g_send, g_ext, g_ss, g_rs, o).wait_send()
        in_copy(f_send, f_ext, f_ss, f_rs, o).wait_send()

    @pl.loop(1, count)
    def _(o):
        d_copy(o).wait_send()

    for n in range(tasks):
        @pl.when(n != task)
        def _():
            back_copy(gi_own, gi_in, gi_ss, gi_rs, n).wait_send()
            back_copy(out_own, out_in, out_ss, out_rs, n).wait_send()


def on_device(features, weight, grad_out, band_width, band_start):
    features = jnp.transpose(features, (0, 2, 1, 3))
    grad_out = jnp.transpose(grad_out, (0, 2, 1, 3))
    members, block, rows, channels = features.shape
    count = lax.axis_size("lon")
    groups = lax.axis_size("ens")
    tasks = members * rows
    lines = groups // 2
    padded = -(-block // 16) * 16
    shard = weight.shape[0]
    piece = shard // 2
    strip_rows = piece // tasks
    vmem = pltpu.VMEM
    dma = pltpu.SemaphoreType.DMA
    field = vmem((tasks, padded, channels), BF)
    ext = vmem((2 * count, padded, channels), BF)
    strip = vmem((K * padded, count * padded), BF)
    wide = vmem((K, tasks, padded, channels), BF)
    scratch = [
        field, field, ext, ext, strip, strip, wide, wide,
        vmem((groups, 2, piece, channels), BF),
        field, field, field, field,
        vmem((lines, 2, 2, piece, channels), F32),
        vmem((lines, 2, piece, channels), BF),
        vmem((lines, 2, piece, channels), BF),
        vmem((lines, 2, piece, channels), BF),
        vmem((lines, 2, piece, channels), BF),
        vmem((2, tasks, strip_rows, channels), BF),
        vmem((2, tasks, strip_rows, channels), BF),
        vmem((count, strip_rows, channels), BF),
        dma((tasks,)), dma((count,)), dma((tasks,)),
        dma((tasks,)), dma((count,)), dma((tasks,)),
        dma((2 * lines,)), dma((groups,)), dma(()), dma(()),
        dma((tasks,)), dma((tasks,)), dma((tasks,)), dma((tasks,)),
        dma((lines + 1,)), dma((lines,)), dma((lines,)), dma((lines,)),
        dma((2 * tasks,)), dma((2, tasks)), dma((count,)), dma((count,)),
    ]
    whole = pl.BlockSpec(memory_space=pltpu.VMEM)
    scalar = pl.BlockSpec(memory_space=pltpu.SMEM)
    output, grad_input, grad_weight = pl.pallas_call(
        functools.partial(kernel, count, groups),
        out_shape=(
            jax.ShapeDtypeStruct(features.shape, BF),
            jax.ShapeDtypeStruct(features.shape, BF),
            jax.ShapeDtypeStruct(weight.shape, F32),
        ),
        in_specs=[whole, whole, whole, scalar, scalar],
        out_specs=(whole, whole, whole),
        scratch_shapes=scratch,
        compiler_params=pltpu.CompilerParams(
            collective_id=0, has_side_effects=True, vmem_limit_bytes=60 * 1024 * 1024
        ),
    )(features, grad_out, weight, band_width, band_start)
    return jnp.transpose(output, (0, 2, 1, 3)), jnp.transpose(grad_input, (0, 2, 1, 3)), grad_weight


def solution(mesh):
    placed = (P("ens", None, "lon", None), P("ens", None), P("ens", None, "lon", None), P(), P())
    return jax.shard_map(
        on_device,
        mesh=mesh,
        in_specs=placed,
        out_specs=(P("ens", None, "lon", None), P("ens", None, "lon", None), P("ens", None)),
        check_vma=False,
    )
```

```python
import functools

import jax
import jax.numpy as jnp
from jax import lax
from jax.experimental import pallas as pl
from jax.experimental.pallas import tpu as pltpu
from jax.sharding import PartitionSpec as P

K = 4
BF = jnp.bfloat16
F32 = jnp.float32


def remote(src, dst, send, recv, lon, ens):
    return pltpu.make_async_remote_copy(
        src_ref=src,
        dst_ref=dst,
        send_sem=send,
        recv_sem=recv,
        device_id={"lon": lon, "ens": ens},
        device_id_type=pl.DeviceIdType.MESH,
    )


def fill_strips(plus, minus, width, start, block, padded, count, flip):
    circle = block * count
    lanes = padded * count // 2
    step = min(128, lanes)
    row = lax.broadcasted_iota(jnp.int32, (padded, step), 0)
    lane = lax.broadcasted_iota(jnp.int32, (padded, step), 1)
    wide = jnp.full((1, step), width.astype(F32), F32)
    scale = 0.5 / jnp.sqrt(wide)
    for first in range(0, lanes, step):
        column = lane + first
        low = first // padded
        part = jnp.full_like(column, low)
        for edge in range(low + 1, (first + step - 1) // padded + 1):
            part = part + (column >= edge * padded).astype(jnp.int32)
        inner = column - part * padded
        place = inner + part * block
        valid = (inner < block) & (row < block)
        near = (row - place if flip else place - row) - start
        near = jnp.where(near < 0, near + circle, near)
        near = jnp.where(near >= circle, near - circle, near)
        far = jnp.where(near >= circle // 2, near - circle // 2, near + circle // 2)
        in_near = valid & (near < width)
        in_far = valid & (far < width)
        at_near = (near.astype(F32) + 0.5) * (K - 1) / wide
        at_far = (far.astype(F32) + 0.5) * (K - 1) / wide
        for k in range(K):
            one = jnp.where(in_near, jnp.maximum(0.0, 1.0 - jnp.abs(at_near - float(k))) * scale, 0.0)
            two = jnp.where(in_far, jnp.maximum(0.0, 1.0 - jnp.abs(at_far - float(k))) * scale, 0.0)
            where = (pl.ds(k * padded, padded), pl.ds(first, step))
            plus[where] = (one + two).astype(BF)
            minus[where] = (one - two).astype(BF)


def spread(block, padded, rows):
    to = lax.broadcasted_iota(jnp.int32, (rows * padded, block * rows), 0)
    source = lax.broadcasted_iota(jnp.int32, (rows * padded, block * rows), 1)
    row = sum((to >= padded * r).astype(jnp.int32) for r in range(1, rows))
    place = to - padded * row
    return ((source == place * rows + row) & (place < block)).astype(F32).astype(BF)


def gather_back(block, padded, rows):
    to = lax.broadcasted_iota(jnp.int32, (block * rows, rows * padded), 0)
    source = lax.broadcasted_iota(jnp.int32, (block * rows, rows * padded), 1)
    place = lax.div(to, rows)
    return (source == (to - place * rows) * padded + place).astype(F32).astype(BF)


def kernel(
    count, groups,
    f_hbm, g_hbm, w_hbm, width_ref, start_ref,
    out_in, gi_in, gw_ref,
    f_ref, g_ref, f_send, g_send, f_ext, g_ext, f_plus, f_minus, g_plus, g_minus, sums, differences, resp, adj, w_all,
    out_own, gi_own,
    turned, gw_own, gw_half, gw_mate, gw_sum, gw_hop, gw_line, gw_part, gw_part_in, gw_full,
    f_ss, f_rs, f_fs, g_ss, g_rs, g_fs, w_ss, w_rs, w_ms, w_mr,
    out_ss, out_rs, gi_ss, gi_rs,
    a_ss, a_rs, b_ss, b_hs, b_rs, c_ss, c_rs, d_ss, d_rs, d_ms, keep_sem, load_sem,
):
    members, block, rows, channels = f_hbm.shape
    padded = f_send.shape[1]
    tasks = members * rows
    lon = lax.axis_index("lon")
    ens = lax.axis_index("ens")
    half = lax.rem(lon, 2)
    task = lax.div(lon, 2)
    mate = lon + 1 - 2 * half
    side = lax.rem(ens, 2)
    line = lax.div(ens, 2)
    lines = groups // 2
    across = ens + 1 - 2 * side
    beside = lon + 2 - 4 * lax.rem(task, 2)

    barrier = pltpu.get_barrier_semaphore()

    def greet(to_lon, to_ens):
        pl.semaphore_signal(barrier, inc=1, device_id={"lon": to_lon, "ens": to_ens}, device_id_type=pl.DeviceIdType.MESH)

    for o in range(1, tasks):
        greet(2 * lax.rem(task + o, tasks) + half, ens)
    greet(mate, ens)
    for o in range(1, lines):
        greet(lon, 2 * lax.rem(line + o, lines) + side)
    for o in range(tasks):
        greet(2 * lax.rem(task + o, tasks) + half, across)

    def stage(ref, buffer, ext):
        for m in range(members):
            flat = ref[m].reshape(block * rows, channels)
            moved = jnp.dot(to_rows, flat, preferred_element_type=F32).astype(BF)
            buffer[pl.ds(m * rows, rows)] = moved.reshape(rows, padded, channels)
        ext[lon] = buffer[task]

    piece = w_all.shape[2]
    load_g = pltpu.make_async_copy(g_hbm, g_ref, load_sem.at[0])
    load_w = [pltpu.make_async_copy(w_hbm.at[pl.ds(i * piece, piece)], w_all.at[ens, i], load_sem.at[1 + i]) for i in range(2)]
    load_f = pltpu.make_async_copy(f_hbm, f_ref, load_sem.at[3])
    for load in (load_g, *load_w, load_f):
        load.start()
    to_rows = spread(block, padded, rows)
    load_g.wait()
    stage(g_ref, g_send, g_ext)
    for load in load_w:
        load.wait()

    pl.semaphore_wait(barrier, 2 * tasks + lines - 1)

    w_across = remote(w_all.at[ens, half], w_all.at[ens, half], w_ss.at[0], w_rs.at[ens], beside, across)

    def along(o):
        return 2 * lax.rem(line + o, lines) + side

    def w_copy(o):
        return remote(w_all.at[ens, half], w_all.at[ens, half], w_ss.at[o], w_rs.at[ens], lon, along(o))

    def w_second(o):
        return remote(w_all.at[across, half], w_all.at[across, half], w_ss.at[lines + o], w_rs.at[across], lon, along(o))

    def w_from(other):
        return remote(w_all.at[other, half], w_all.at[other, half], w_ss.at[0], w_rs.at[other], lon, other)

    def in_copy(buffer, ext, ss, rs, o):
        q = lax.rem(task + o, tasks)
        return remote(buffer.at[q], ext.at[lon], ss.at[o], rs.at[lon], 2 * q + half, ens)

    def in_from(ext, ss, rs, o):
        slot = 2 * lax.rem(task + tasks - o, tasks) + half
        return remote(ext.at[slot], ext.at[slot], ss.at[o], rs.at[slot], slot, ens)

    def forward(ext, fs, rs, o):
        slot = 2 * lax.rem(task + tasks - o, tasks) + half
        return remote(ext.at[slot], ext.at[slot], fs.at[o], rs.at[slot], mate, ens)

    def forwarded(ext, fs, rs, o):
        slot = 2 * lax.rem(task + tasks - o, tasks) + 1 - half
        return remote(ext.at[slot], ext.at[slot], fs.at[o], rs.at[slot], mate, ens)

    @pl.loop(1, tasks)
    def _(o):
        in_copy(g_send, g_ext, g_ss, g_rs, o).start()

    w_across.start()

    @pl.loop(1, lines)
    def _(o):
        w_copy(o).start()

    forward(g_ext, g_fs, g_rs, 0).start()
    load_f.wait()
    stage(f_ref, f_send, f_ext)
    forward(f_ext, f_fs, f_rs, 0).start()

    remote(w_all.at[across, half], w_all.at[across, half], w_ss.at[0], w_rs.at[across], beside, across).wait_recv()

    @pl.loop(1, lines)
    def _(o):
        w_second(o).start()

    row = lax.rem(task, rows)
    fill_strips(g_plus, g_minus, width_ref[row], start_ref[row], block, padded, count, True)

    @pl.loop(1, tasks)
    def _(o):
        in_copy(g_send, g_ext, g_ss, g_rs, o).wait_send()
        in_copy(f_send, f_ext, f_ss, f_rs, o).start()

    fill_strips(f_plus, f_minus, width_ref[row], start_ref[row], block, padded, count, False)

    def pass_on(ext, ss, fs, rs):
        @pl.loop(1, tasks)
        def _(o):
            in_from(ext, ss, rs, o).wait_recv()
            forward(ext, fs, rs, o).start()

    def complete(ext, fs, rs):
        @pl.loop(0, tasks)
        def _(o):
            forwarded(ext, fs, rs, o).wait_recv()

        @pl.loop(0, tasks)
        def _(b):
            one = ext[b].astype(F32)
            two = ext[tasks + b].astype(F32)
            both = (one + two).astype(BF)
            apart = one - two
            sums[b] = both
            sums[tasks + b] = both
            differences[b] = apart.astype(BF)
            differences[tasks + b] = (-apart).astype(BF)

    def convolve(plus, minus, result):
        @pl.loop(0, tasks // 2)
        def _(n):
            window = pl.ds(2 * n + half, tasks)
            both = jnp.dot(plus[...], sums[window].reshape(tasks * padded, channels), preferred_element_type=F32)
            apart = jnp.dot(minus[...], differences[window].reshape(tasks * padded, channels), preferred_element_type=F32)
            near = (both + apart).astype(BF)
            far = (both - apart).astype(BF)
            for k in range(K):
                result[k, n] = near[k * padded:(k + 1) * padded]
                result[k, tasks // 2 + n] = far[k * padded:(k + 1) * padded]

    def weight_of(k):
        return w_all[pl.ds(2 * k, 2)].reshape(channels, channels)

    def back_copy(own, into, ss, rs, n):
        return remote(own.at[n], into.at[task], ss.at[n], rs.at[task], 2 * n + half, ens)

    def back_from(own, into, ss, rs, n):
        return remote(own.at[n], into.at[n], ss.at[n], rs.at[n], 2 * n + half, ens)

    def mix(source, own, c, flip):
        chunk = tasks // 2
        total = None
        for k in range(K):
            part = source[k, pl.ds(c * chunk, chunk)].reshape(chunk * padded, channels)
            dims = (((1,), (1 if flip else 0,)), ((), ()))
            term = lax.dot_general(part, weight_of(k), dims, preferred_element_type=F32)
            total = term if total is None else total + term
        own[pl.ds(c * chunk, chunk)] = total.astype(BF).reshape(chunk, padded, channels)

    def send_back(own, into, ss, rs, c):
        chunk = tasks // 2
        for n in range(c * chunk, (c + 1) * chunk):
            @pl.when(n != task)
            def _():
                back_copy(own, into, ss, rs, n).start()

    pass_on(g_ext, g_ss, g_fs, g_rs)
    complete(g_ext, g_fs, g_rs)

    def w_mate(e):
        return remote(w_all.at[e, half], w_all.at[e, half], w_ms.at[e], w_mr.at[e], mate, ens)

    def w_mate_from(e):
        return remote(w_all.at[e, 1 - half], w_all.at[e, 1 - half], w_ms.at[e], w_mr.at[e], mate, ens)

    @pl.loop(1, lines)
    def _(o):
        w_from(along(o)).wait_recv()
        w_mate(along(o)).start()

    w_mate(across).start()
    convolve(g_plus, g_minus, adj)

    @pl.loop(1, lines)
    def _(o):
        w_from(along(o) + 1 - 2 * side).wait_recv()
        w_mate(along(o) + 1 - 2 * side).start()

    @pl.loop(1, groups)
    def _(o):
        w_mate_from(lax.rem(ens + o, groups)).wait_recv()

    for c in range(2):
        mix(adj, gi_own, c, True)
        send_back(gi_own, gi_in, gi_ss, gi_rs, c)

    pass_on(f_ext, f_ss, f_fs, f_rs)
    own_rows = jnp.concatenate([f_ext[2 * n + half] for n in range(tasks)], axis=0)
    turned[...] = own_rows.T.reshape(turned.shape)

    def a_copy(to):
        return remote(gw_half.at[to], gw_mate.at[to], a_ss.at[to], a_rs.at[to], mate, ens)

    def terms(to, which):
        left = turned[:, which].reshape(2 * piece, tasks * padded)
        right = adj[to].reshape(tasks * padded, channels)
        return jnp.dot(left, right, preferred_element_type=F32).reshape(2, piece, channels)

    order = [lax.rem(line + o, lines) for o in (2, 1, 3, 0)]
    for to in order:
        gw_half[to] = terms(to, 1 - half).astype(BF)
        a_copy(to).start()
    for to in order:
        gw_own[to] = terms(to, half)

    ahead = lax.rem(line + 1, lines)
    back = lax.rem(line + lines - 1, lines)
    opposite = lax.rem(line + 2, lines)
    ways = ((0, ahead, back), (1, back, ahead))

    def chip_sum(to, i):
        return gw_own[to, i] + gw_mate[to, i].astype(F32)

    def hop(i):
        _, to, _ = ways[i]
        return remote(gw_sum.at[opposite, i], gw_hop.at[i], b_ss.at[0, i], b_hs.at[i], lon, 2 * to + side)

    def plain(i):
        _, to, _ = ways[i]
        return remote(gw_sum.at[to, 1 - i], gw_line.at[i, 1 - i], b_ss.at[1, i], b_rs.at[i, 1 - i], lon, 2 * to + side)

    def added(i):
        _, to, _ = ways[i]
        return remote(gw_sum.at[to, i], gw_line.at[i, i], b_ss.at[2, i], b_rs.at[i, i], lon, 2 * to + side)

    a_copy(opposite).wait_recv()
    for i in range(2):
        gw_sum[opposite, i] = chip_sum(opposite, i).astype(BF)
        hop(i).start()
    for i, to, _ in ways:
        a_copy(to).wait_recv()
        gw_sum[to, 1 - i] = chip_sum(to, 1 - i).astype(BF)
        plain(i).start()
    a_copy(line).wait_recv()

    complete(f_ext, f_fs, f_rs)
    convolve(f_plus, f_minus, resp)

    for i, to, _ in ways:
        hop(i).wait_recv()
        gw_sum[to, i] = (chip_sum(to, i) + gw_hop[i].astype(F32)).astype(BF)
        added(i).start()

    mix(resp, out_own, 0, False)
    send_back(out_own, out_in, out_ss, out_rs, 0)
    mix(resp, out_own, 1, False)

    for i in range(2):
        plain(i).wait_recv()
        added(i).wait_recv()
    for s in range(2):
        total = chip_sum(line, s) + gw_line[0, s].astype(F32) + gw_line[1, s].astype(F32)
        gw_part[s] = total.astype(BF).reshape(gw_part.shape[1:])

    def c_place(o):
        s = lax.rem(side + lax.div(o, tasks), 2)
        return s, lax.rem(task + lax.rem(o, tasks), tasks)

    def c_copy(o):
        s, q = c_place(o)
        return remote(gw_part.at[s, q], gw_part_in.at[side, task], c_ss.at[o], c_rs.at[side, task], 2 * q + half, 2 * line + s)

    def c_from(o):
        s, q = c_place(o)
        return remote(gw_part.at[s, q], gw_part_in.at[s, q], c_ss.at[o], c_rs.at[s, q], 2 * q + half, 2 * line + s)

    @pl.loop(1, 2 * tasks)
    def _(o):
        c_copy(o).start()

    send_back(out_own, out_in, out_ss, out_rs, 1)
    gw_part_in[side, task] = gw_part[side, task]

    def d_copy(o):
        return remote(gw_full.at[lon], gw_full.at[lon], d_ss.at[o], d_rs.at[lon], 2 * lax.rem(task + o, tasks) + half, ens)

    def d_from(o):
        other = 2 * lax.rem(task + tasks - o, tasks) + half
        return remote(gw_full.at[other], gw_full.at[other], d_ss.at[o], d_rs.at[other], other, ens)

    def d_mate(o):
        other = 2 * lax.rem(task + tasks - o, tasks) + half
        return remote(gw_full.at[other], gw_full.at[other], d_ms.at[o], d_rs.at[other], mate, ens)

    def d_mate_from(o):
        other = 2 * lax.rem(task + tasks - o, tasks) + 1 - half
        return remote(gw_full.at[other], gw_full.at[other], d_ms.at[o], d_rs.at[other], mate, ens)

    @pl.loop(1, 2 * tasks)
    def _(o):
        c_from(o).wait_recv()

    total = None
    for e in range(2):
        for q in range(tasks):
            term = gw_part_in[e, q].astype(F32)
            total = term if total is None else total + term
    gw_full[lon] = total.astype(BF)

    @pl.loop(1, tasks)
    def _(o):
        d_copy(o).start()

    d_mate(0).start()

    keep_gi = pltpu.make_async_copy(gi_own.at[task], gi_in.at[task], keep_sem.at[0])
    keep_out = pltpu.make_async_copy(out_own.at[task], out_in.at[task], keep_sem.at[1])
    keep_gi.start()
    keep_out.start()

    @pl.loop(1, tasks)
    def _(o):
        d_from(o).wait_recv()
        d_mate(o).start()

    @pl.loop(0, tasks)
    def _(o):
        d_mate_from(o).wait_recv()

    gw_ref[...] = gw_full[...]

    for n in range(tasks):
        @pl.when(n != task)
        def _():
            back_from(gi_own, gi_in, gi_ss, gi_rs, n).wait_recv()
            back_from(out_own, out_in, out_ss, out_rs, n).wait_recv()

    keep_gi.wait()
    keep_out.wait()

    w_across.wait_send()

    @pl.loop(1, lines)
    def _(o):
        w_copy(o).wait_send()
        w_second(o).wait_send()

    @pl.loop(1, groups)
    def _(o):
        w_mate(lax.rem(ens + o, groups)).wait_send()

    @pl.loop(0, lines)
    def _(o):
        a_copy(o).wait_send()

    for i in range(2):
        hop(i).wait_send()
        plain(i).wait_send()
        added(i).wait_send()

    @pl.loop(1, 2 * tasks)
    def _(o):
        c_copy(o).wait_send()

    @pl.loop(0, tasks)
    def _(o):
        forward(g_ext, g_fs, g_rs, o).wait_send()
        forward(f_ext, f_fs, f_rs, o).wait_send()

    @pl.loop(1, tasks)
    def _(o):
        in_copy(f_send, f_ext, f_ss, f_rs, o).wait_send()

    @pl.loop(1, tasks)
    def _(o):
        d_copy(o).wait_send()

    @pl.loop(0, tasks)
    def _(o):
        d_mate(o).wait_send()

    for n in range(tasks):
        @pl.when(n != task)
        def _():
            back_copy(gi_own, gi_in, gi_ss, gi_rs, n).wait_send()
            back_copy(out_own, out_in, out_ss, out_rs, n).wait_send()


def lay_out(block, out_hbm, gi_hbm, gw_hbm, out_ref, gi_ref, gw_ref, out_in, gi_in, gw_in, out_done, gi_done, gw_done, sems, done_sems):
    tasks, padded, channels = out_hbm.shape
    members, _, rows, _ = out_ref.shape
    loads = []
    for i, (source, into) in enumerate(((gi_hbm, gi_in), (out_hbm, out_in))):
        for m in range(members):
            part = pl.ds(m * rows, rows)
            loads.append(pltpu.make_async_copy(source.at[part], into.at[part], sems.at[i * members + m]))
    loads.append(pltpu.make_async_copy(gw_hbm, gw_in, sems.at[2 * members]))
    for load in loads:
        load.start()
    to_places = gather_back(block, padded, rows)
    stores = []
    for i, (into, ready, ref) in enumerate(((gi_in, gi_done, gi_ref), (out_in, out_done, out_ref))):
        for m in range(members):
            loads[i * members + m].wait()
            flat = into[pl.ds(m * rows, rows)].reshape(rows * padded, channels)
            moved = jnp.dot(to_places, flat, preferred_element_type=F32).astype(BF)
            ready[m] = moved.reshape(block, rows, channels)
            stores.append(pltpu.make_async_copy(ready.at[m], ref.at[m], done_sems.at[i * members + m]))
            stores[-1].start()
    loads[-1].wait()
    strip_rows = gw_in.shape[1]
    for q in range(tasks):
        for s in range(2):
            gw_done[pl.ds((s * tasks + q) * strip_rows, strip_rows), :] = gw_in[2 * q + s].astype(F32)
    stores.append(pltpu.make_async_copy(gw_done, gw_ref, done_sems.at[2 * members]))
    stores[-1].start()
    for store in stores:
        store.wait()


def on_device(features, weight, grad_out, band_width, band_start):
    features = jnp.transpose(features, (0, 2, 1, 3))
    grad_out = jnp.transpose(grad_out, (0, 2, 1, 3))
    members, block, rows, channels = features.shape
    count = lax.axis_size("lon")
    groups = lax.axis_size("ens")
    tasks = members * rows
    lines = groups // 2
    padded = -(-block // 16) * 16
    shard = weight.shape[0]
    piece = shard // 2
    strip_rows = piece // tasks
    vmem = pltpu.VMEM
    dma = pltpu.SemaphoreType.DMA
    field = vmem((tasks, padded, channels), BF)
    ext = vmem((count, padded, channels), BF)
    strip = vmem((K * padded, tasks * padded), BF)
    wide = vmem((K, tasks, padded, channels), BF)
    scratch = [
        vmem(features.shape, BF), vmem(features.shape, BF), field, field, ext, ext, strip, strip, strip, strip, ext, ext, wide, wide,
        vmem((groups, 2, piece, channels), BF),
        field, field,
        vmem((2, 2, piece, tasks * padded), BF),
        vmem((lines, 2, piece, channels), F32),
        vmem((lines, 2, piece, channels), BF),
        vmem((lines, 2, piece, channels), BF),
        vmem((lines, 2, piece, channels), BF),
        vmem((2, piece, channels), BF),
        vmem((2, 2, piece, channels), BF),
        vmem((2, tasks, strip_rows, channels), BF),
        vmem((2, tasks, strip_rows, channels), BF),
        vmem((count, strip_rows, channels), BF),
        dma((tasks,)), dma((count,)), dma((tasks,)),
        dma((tasks,)), dma((count,)), dma((tasks,)),
        dma((2 * lines,)), dma((groups,)), dma((groups,)), dma((groups,)),
        dma((tasks,)), dma((tasks,)), dma((tasks,)), dma((tasks,)),
        dma((lines,)), dma((lines,)), dma((3, 2)), dma((2,)), dma((2, 2)),
        dma((2 * tasks,)), dma((2, tasks)), dma((tasks,)), dma((count,)), dma((tasks,)), dma((2,)), dma((4,)),
    ]
    whole = pl.BlockSpec(memory_space=pltpu.VMEM)
    scalar = pl.BlockSpec(memory_space=pltpu.SMEM)
    any_place = pl.BlockSpec(memory_space=pl.ANY)
    back = jax.ShapeDtypeStruct((tasks, padded, channels), BF)
    parts = pl.pallas_call(
        functools.partial(kernel, count, groups),
        out_shape=(back, back, jax.ShapeDtypeStruct((count, strip_rows, channels), BF)),
        in_specs=[any_place, any_place, any_place, scalar, scalar],
        out_specs=(any_place, any_place, whole),
        scratch_shapes=scratch,
        compiler_params=pltpu.CompilerParams(
            collective_id=0, has_side_effects=True, vmem_limit_bytes=60 * 1024 * 1024
        ),
    )(features, grad_out, weight, band_width, band_start)
    output, grad_input, grad_weight = pl.pallas_call(
        functools.partial(lay_out, block),
        out_shape=(
            jax.ShapeDtypeStruct(features.shape, BF),
            jax.ShapeDtypeStruct(features.shape, BF),
            jax.ShapeDtypeStruct(weight.shape, F32),
        ),
        in_specs=[any_place] * 3,
        out_specs=(any_place,) * 3,
        scratch_shapes=[
            field, field, vmem((count, strip_rows, channels), BF),
            vmem(features.shape, BF), vmem(features.shape, BF), vmem(weight.shape, F32),
            dma((2 * members + 1,)), dma((2 * members + 1,)),
        ],
        compiler_params=pltpu.CompilerParams(vmem_limit_bytes=60 * 1024 * 1024),
    )(*parts)
    return jnp.transpose(output, (0, 2, 1, 3)), jnp.transpose(grad_input, (0, 2, 1, 3)), grad_weight


def solution(mesh):
    placed = (P("ens", None, "lon", None), P("ens", None), P("ens", None, "lon", None), P(), P())
    return jax.shard_map(
        on_device,
        mesh=mesh,
        in_specs=placed,
        out_specs=(P("ens", None, "lon", None), P("ens", None, "lon", None), P("ens", None)),
        check_vma=False,
    )
```

```python
import functools

import jax
import jax.numpy as jnp
from jax import lax
from jax.experimental import pallas as pl
from jax.experimental.pallas import tpu as pltpu
from jax.sharding import PartitionSpec as P

K = 4
BF = jnp.bfloat16
F32 = jnp.float32


def remote(src, dst, send, recv, lon, ens):
    return pltpu.make_async_remote_copy(
        src_ref=src,
        dst_ref=dst,
        send_sem=send,
        recv_sem=recv,
        device_id={"lon": lon, "ens": ens},
        device_id_type=pl.DeviceIdType.MESH,
    )


def fill_strips(plus, minus, width, start, block, padded, count, flip):
    circle = block * count
    lanes = padded * count // 2
    step = min(128, lanes)
    row = lax.broadcasted_iota(jnp.int32, (padded, step), 0)
    lane = lax.broadcasted_iota(jnp.int32, (padded, step), 1)
    wide = jnp.full((1, step), width.astype(F32), F32)
    scale = 0.5 / jnp.sqrt(wide)
    for first in range(0, lanes, step):
        column = lane + first
        low = first // padded
        part = jnp.full_like(column, low)
        for edge in range(low + 1, (first + step - 1) // padded + 1):
            part = part + (column >= edge * padded).astype(jnp.int32)
        inner = column - part * padded
        place = inner + part * block
        valid = (inner < block) & (row < block)
        near = (row - place if flip else place - row) - start
        near = jnp.where(near < 0, near + circle, near)
        near = jnp.where(near >= circle, near - circle, near)
        far = jnp.where(near >= circle // 2, near - circle // 2, near + circle // 2)
        in_near = valid & (near < width)
        in_far = valid & (far < width)
        at_near = (near.astype(F32) + 0.5) * (K - 1) / wide
        at_far = (far.astype(F32) + 0.5) * (K - 1) / wide
        for k in range(K):
            one = jnp.where(in_near, jnp.maximum(0.0, 1.0 - jnp.abs(at_near - float(k))) * scale, 0.0)
            two = jnp.where(in_far, jnp.maximum(0.0, 1.0 - jnp.abs(at_far - float(k))) * scale, 0.0)
            where = (pl.ds(k * padded, padded), pl.ds(first, step))
            plus[where] = (one + two).astype(BF)
            minus[where] = (one - two).astype(BF)


def spread(block, padded, rows):
    to = lax.broadcasted_iota(jnp.int32, (rows * padded, block * rows), 0)
    source = lax.broadcasted_iota(jnp.int32, (rows * padded, block * rows), 1)
    row = sum((to >= padded * r).astype(jnp.int32) for r in range(1, rows))
    place = to - padded * row
    return ((source == place * rows + row) & (place < block)).astype(F32).astype(BF)


def gather_back(block, padded, rows):
    to = lax.broadcasted_iota(jnp.int32, (block * rows, rows * padded), 0)
    source = lax.broadcasted_iota(jnp.int32, (block * rows, rows * padded), 1)
    place = lax.div(to, rows)
    return (source == (to - place * rows) * padded + place).astype(F32).astype(BF)


def kernel(
    count, groups,
    f_hbm, g_hbm, w_hbm, width_ref, start_ref,
    out_ref, gi_ref, gw_ref,
    f_ref, g_ref, f_send, g_send, f_ext, g_ext, f_plus, f_minus, g_plus, g_minus, sums, differences, resp, adj, w_all,
    out_own, gi_own, out_in, gi_in, out_done, gi_done, gw_done,
    turned, gw_own, gw_half, gw_mate, gw_sum, gw_hop, gw_line, gw_part, gw_part_in, gw_full,
    f_ss, f_rs, f_fs, g_ss, g_rs, g_fs, w_ss, w_rs, w_ms, w_mr,
    out_ss, out_rs, gi_ss, gi_rs,
    a_ss, a_rs, b_ss, b_hs, b_rs, c_ss, c_rs, d_ss, d_rs, d_ms, keep_sem, load_sem,
):
    members, block, rows, channels = f_hbm.shape
    padded = f_send.shape[1]
    tasks = members * rows
    lon = lax.axis_index("lon")
    ens = lax.axis_index("ens")
    half = lax.rem(lon, 2)
    task = lax.div(lon, 2)
    mate = lon + 1 - 2 * half
    side = lax.rem(ens, 2)
    line = lax.div(ens, 2)
    lines = groups // 2
    across = ens + 1 - 2 * side
    beside = lon + 2 - 4 * lax.rem(task, 2)

    barrier = pltpu.get_barrier_semaphore()

    def greet(to_lon, to_ens):
        pl.semaphore_signal(barrier, inc=1, device_id={"lon": to_lon, "ens": to_ens}, device_id_type=pl.DeviceIdType.MESH)

    for o in range(1, tasks):
        greet(2 * lax.rem(task + o, tasks) + half, ens)
    greet(mate, ens)
    for o in range(1, lines):
        greet(lon, 2 * lax.rem(line + o, lines) + side)
    greet(beside, across)

    def stage(ref, buffer, ext):
        for m in range(members):
            flat = ref[m].reshape(block * rows, channels)
            moved = jnp.dot(to_rows, flat, preferred_element_type=F32).astype(BF)
            buffer[pl.ds(m * rows, rows)] = moved.reshape(rows, padded, channels)
        ext[lon] = buffer[task]

    piece = w_all.shape[2]
    load_g = pltpu.make_async_copy(g_hbm, g_ref, load_sem.at[0])
    load_w = [pltpu.make_async_copy(w_hbm.at[pl.ds(i * piece, piece)], w_all.at[ens, i], load_sem.at[1 + i]) for i in range(2)]
    load_f = pltpu.make_async_copy(f_hbm, f_ref, load_sem.at[3])
    for load in (load_g, *load_w, load_f):
        load.start()
    to_rows = spread(block, padded, rows)
    load_g.wait()
    stage(g_ref, g_send, g_ext)
    for load in load_w:
        load.wait()

    pl.semaphore_wait(barrier, tasks + lines)

    w_across = remote(w_all.at[ens, half], w_all.at[ens, half], w_ss.at[0], w_rs.at[ens], beside, across)

    def along(o):
        return 2 * lax.rem(line + o, lines) + side

    def w_copy(o):
        return remote(w_all.at[ens, half], w_all.at[ens, half], w_ss.at[o], w_rs.at[ens], lon, along(o))

    def w_second(o):
        return remote(w_all.at[across, half], w_all.at[across, half], w_ss.at[lines + o], w_rs.at[across], lon, along(o))

    def w_from(other):
        return remote(w_all.at[other, half], w_all.at[other, half], w_ss.at[0], w_rs.at[other], lon, other)

    def in_copy(buffer, ext, ss, rs, o):
        q = lax.rem(task + o, tasks)
        return remote(buffer.at[q], ext.at[lon], ss.at[o], rs.at[lon], 2 * q + half, ens)

    def in_from(ext, ss, rs, o):
        slot = 2 * lax.rem(task + tasks - o, tasks) + half
        return remote(ext.at[slot], ext.at[slot], ss.at[o], rs.at[slot], slot, ens)

    def forward(ext, fs, rs, o):
        slot = 2 * lax.rem(task + tasks - o, tasks) + half
        return remote(ext.at[slot], ext.at[slot], fs.at[o], rs.at[slot], mate, ens)

    def forwarded(ext, fs, rs, o):
        slot = 2 * lax.rem(task + tasks - o, tasks) + 1 - half
        return remote(ext.at[slot], ext.at[slot], fs.at[o], rs.at[slot], mate, ens)

    @pl.loop(1, tasks)
    def _(o):
        in_copy(g_send, g_ext, g_ss, g_rs, o).start()

    w_across.start()

    @pl.loop(1, lines)
    def _(o):
        w_copy(o).start()

    forward(g_ext, g_fs, g_rs, 0).start()
    load_f.wait()
    stage(f_ref, f_send, f_ext)
    forward(f_ext, f_fs, f_rs, 0).start()

    remote(w_all.at[across, half], w_all.at[across, half], w_ss.at[0], w_rs.at[across], beside, across).wait_recv()

    @pl.loop(1, lines)
    def _(o):
        w_second(o).start()

    row = lax.rem(task, rows)
    fill_strips(g_plus, g_minus, width_ref[row], start_ref[row], block, padded, count, True)

    @pl.loop(1, tasks)
    def _(o):
        in_copy(g_send, g_ext, g_ss, g_rs, o).wait_send()
        in_copy(f_send, f_ext, f_ss, f_rs, o).start()

    fill_strips(f_plus, f_minus, width_ref[row], start_ref[row], block, padded, count, False)

    def pass_on(ext, ss, fs, rs):
        @pl.loop(1, tasks)
        def _(o):
            in_from(ext, ss, rs, o).wait_recv()
            forward(ext, fs, rs, o).start()

    def complete(ext, fs, rs):
        @pl.loop(0, tasks)
        def _(o):
            forwarded(ext, fs, rs, o).wait_recv()

        @pl.loop(0, tasks)
        def _(b):
            one = ext[b].astype(F32)
            two = ext[tasks + b].astype(F32)
            both = (one + two).astype(BF)
            apart = one - two
            sums[b] = both
            sums[tasks + b] = both
            differences[b] = apart.astype(BF)
            differences[tasks + b] = (-apart).astype(BF)

    def convolve(plus, minus, result):
        @pl.loop(0, tasks // 2)
        def _(n):
            window = pl.ds(2 * n + half, tasks)
            both = jnp.dot(plus[...], sums[window].reshape(tasks * padded, channels), preferred_element_type=F32)
            apart = jnp.dot(minus[...], differences[window].reshape(tasks * padded, channels), preferred_element_type=F32)
            near = (both + apart).astype(BF)
            far = (both - apart).astype(BF)
            for k in range(K):
                result[k, n] = near[k * padded:(k + 1) * padded]
                result[k, tasks // 2 + n] = far[k * padded:(k + 1) * padded]

    def weight_of(k):
        return w_all[pl.ds(2 * k, 2)].reshape(channels, channels)

    def back_copy(own, into, ss, rs, n):
        return remote(own.at[n], into.at[task], ss.at[n], rs.at[task], 2 * n + half, ens)

    def back_from(own, into, ss, rs, n):
        return remote(own.at[n], into.at[n], ss.at[n], rs.at[n], 2 * n + half, ens)

    def mix(source, own, c, flip):
        chunk = tasks // 2
        total = None
        for k in range(K):
            part = source[k, pl.ds(c * chunk, chunk)].reshape(chunk * padded, channels)
            dims = (((1,), (1 if flip else 0,)), ((), ()))
            term = lax.dot_general(part, weight_of(k), dims, preferred_element_type=F32)
            total = term if total is None else total + term
        own[pl.ds(c * chunk, chunk)] = total.astype(BF).reshape(chunk, padded, channels)

    def send_back(own, into, ss, rs, c):
        chunk = tasks // 2
        for n in range(c * chunk, (c + 1) * chunk):
            @pl.when(n != task)
            def _():
                back_copy(own, into, ss, rs, n).start()

    pass_on(g_ext, g_ss, g_fs, g_rs)
    complete(g_ext, g_fs, g_rs)

    def w_mate(e):
        return remote(w_all.at[e, half], w_all.at[e, half], w_ms.at[e], w_mr.at[e], mate, ens)

    def w_mate_from(e):
        return remote(w_all.at[e, 1 - half], w_all.at[e, 1 - half], w_ms.at[e], w_mr.at[e], mate, ens)

    @pl.loop(1, lines)
    def _(o):
        w_from(along(o)).wait_recv()
        w_mate(along(o)).start()

    w_mate(across).start()
    convolve(g_plus, g_minus, adj)

    @pl.loop(1, lines)
    def _(o):
        w_from(along(o) + 1 - 2 * side).wait_recv()
        w_mate(along(o) + 1 - 2 * side).start()

    @pl.loop(1, groups)
    def _(o):
        w_mate_from(lax.rem(ens + o, groups)).wait_recv()

    for c in range(2):
        mix(adj, gi_own, c, True)
        send_back(gi_own, gi_in, gi_ss, gi_rs, c)

    pass_on(f_ext, f_ss, f_fs, f_rs)
    own_rows = jnp.concatenate([f_ext[2 * n + half] for n in range(tasks)], axis=0)
    turned[...] = own_rows.T.reshape(turned.shape)

    def a_copy(to):
        return remote(gw_half.at[to], gw_mate.at[to], a_ss.at[to], a_rs.at[to], mate, ens)

    def terms(to, which):
        left = turned[:, which].reshape(2 * piece, tasks * padded)
        right = adj[to].reshape(tasks * padded, channels)
        return jnp.dot(left, right, preferred_element_type=F32).reshape(2, piece, channels)

    order = [lax.rem(line + o, lines) for o in (2, 1, 3, 0)]
    for to in order[:2]:
        gw_half[to] = terms(to, 1 - half).astype(BF)
        a_copy(to).start()
    gw_own[order[0]] = terms(order[0], half)

    ahead = lax.rem(line + 1, lines)
    back = lax.rem(line + lines - 1, lines)
    opposite = lax.rem(line + 2, lines)
    ways = ((0, ahead, back), (1, back, ahead))

    def chip_sum(to, i):
        return gw_own[to, i] + gw_mate[to, i].astype(F32)

    def hop(i):
        _, to, _ = ways[i]
        return remote(gw_sum.at[opposite, i], gw_hop.at[i], b_ss.at[0, i], b_hs.at[i], lon, 2 * to + side)

    def plain(i):
        _, to, _ = ways[i]
        return remote(gw_sum.at[to, 1 - i], gw_line.at[i, 1 - i], b_ss.at[1, i], b_rs.at[i, 1 - i], lon, 2 * to + side)

    def added(i):
        _, to, _ = ways[i]
        return remote(gw_sum.at[to, i], gw_line.at[i, i], b_ss.at[2, i], b_rs.at[i, i], lon, 2 * to + side)

    a_copy(opposite).wait_recv()
    for i in range(2):
        gw_sum[opposite, i] = chip_sum(opposite, i).astype(BF)
        hop(i).start()
    for to in order[2:]:
        gw_half[to] = terms(to, 1 - half).astype(BF)
        a_copy(to).start()
    for to in order[1:]:
        gw_own[to] = terms(to, half)
    for i, to, _ in ways:
        a_copy(to).wait_recv()
        gw_sum[to, 1 - i] = chip_sum(to, 1 - i).astype(BF)
        plain(i).start()
    a_copy(line).wait_recv()

    complete(f_ext, f_fs, f_rs)
    convolve(f_plus, f_minus, resp)

    for i, to, _ in ways:
        hop(i).wait_recv()
        gw_sum[to, i] = (chip_sum(to, i) + gw_hop[i].astype(F32)).astype(BF)
        added(i).start()

    mix(resp, out_own, 0, False)
    send_back(out_own, out_in, out_ss, out_rs, 0)
    mix(resp, out_own, 1, False)

    for i in range(2):
        plain(i).wait_recv()
        added(i).wait_recv()
    for s in range(2):
        total = chip_sum(line, s) + gw_line[0, s].astype(F32) + gw_line[1, s].astype(F32)
        gw_part[s] = total.astype(BF).reshape(gw_part.shape[1:])

    def c_place(o):
        s = lax.rem(side + lax.div(o, tasks), 2)
        return s, lax.rem(task + lax.rem(o, tasks), tasks)

    def c_copy(o):
        s, q = c_place(o)
        return remote(gw_part.at[s, q], gw_part_in.at[side, task], c_ss.at[o], c_rs.at[side, task], 2 * q + half, 2 * line + s)

    def c_from(o):
        s, q = c_place(o)
        return remote(gw_part.at[s, q], gw_part_in.at[s, q], c_ss.at[o], c_rs.at[s, q], 2 * q + half, 2 * line + s)

    @pl.loop(1, 2 * tasks)
    def _(o):
        c_copy(o).start()

    send_back(out_own, out_in, out_ss, out_rs, 1)
    gw_part_in[side, task] = gw_part[side, task]

    def d_copy(o):
        return remote(gw_full.at[lon], gw_full.at[lon], d_ss.at[o], d_rs.at[lon], 2 * lax.rem(task + o, tasks) + half, ens)

    def d_from(o):
        other = 2 * lax.rem(task + tasks - o, tasks) + half
        return remote(gw_full.at[other], gw_full.at[other], d_ss.at[o], d_rs.at[other], other, ens)

    def d_mate(o):
        other = 2 * lax.rem(task + tasks - o, tasks) + half
        return remote(gw_full.at[other], gw_full.at[other], d_ms.at[o], d_rs.at[other], mate, ens)

    def d_mate_from(o):
        other = 2 * lax.rem(task + tasks - o, tasks) + 1 - half
        return remote(gw_full.at[other], gw_full.at[other], d_ms.at[o], d_rs.at[other], mate, ens)

    def finish(ref, done, own, into, ss, rs, which):
        into[task] = own[task]
        keeps = []
        for m in range(members):
            for q in range(m * rows, (m + 1) * rows):
                @pl.when(q != task)
                def _():
                    back_from(own, into, ss, rs, q).wait_recv()
            flat = into[pl.ds(m * rows, rows)].reshape(rows * padded, channels)
            moved = jnp.dot(to_places, flat, preferred_element_type=F32).astype(BF)
            done[m] = moved.reshape(block, rows, channels)
            keeps.append(pltpu.make_async_copy(done.at[m], ref.at[m], keep_sem.at[which * members + m]))
            keeps[-1].start()
        return keeps

    to_places = gather_back(block, padded, rows)
    keep_gi = finish(gi_ref, gi_done, gi_own, gi_in, gi_ss, gi_rs, 0)

    @pl.loop(1, 2 * tasks)
    def _(o):
        c_from(o).wait_recv()

    total = None
    for e in range(2):
        for q in range(tasks):
            term = gw_part_in[e, q].astype(F32)
            total = term if total is None else total + term
    gw_full[lon] = total.astype(BF)

    @pl.loop(1, tasks)
    def _(o):
        d_copy(o).start()

    d_mate(0).start()

    keep_out = finish(out_ref, out_done, out_own, out_in, out_ss, out_rs, 1)

    @pl.loop(1, tasks)
    def _(o):
        d_from(o).wait_recv()
        d_mate(o).start()

    @pl.loop(0, tasks)
    def _(o):
        d_mate_from(o).wait_recv()

    strip_rows = gw_full.shape[1]
    for q in range(tasks):
        for s in range(2):
            gw_done[pl.ds((s * tasks + q) * strip_rows, strip_rows), :] = gw_full[2 * q + s].astype(F32)
    keep_gw = pltpu.make_async_copy(gw_done, gw_ref, keep_sem.at[2 * members])
    keep_gw.start()
    for keep in (*keep_gi, *keep_out, keep_gw):
        keep.wait()

    w_across.wait_send()

    @pl.loop(1, lines)
    def _(o):
        w_copy(o).wait_send()
        w_second(o).wait_send()

    @pl.loop(1, groups)
    def _(o):
        w_mate(lax.rem(ens + o, groups)).wait_send()

    @pl.loop(0, lines)
    def _(o):
        a_copy(o).wait_send()

    for i in range(2):
        hop(i).wait_send()
        plain(i).wait_send()
        added(i).wait_send()

    @pl.loop(1, 2 * tasks)
    def _(o):
        c_copy(o).wait_send()

    @pl.loop(0, tasks)
    def _(o):
        forward(g_ext, g_fs, g_rs, o).wait_send()
        forward(f_ext, f_fs, f_rs, o).wait_send()

    @pl.loop(1, tasks)
    def _(o):
        in_copy(f_send, f_ext, f_ss, f_rs, o).wait_send()

    @pl.loop(1, tasks)
    def _(o):
        d_copy(o).wait_send()

    @pl.loop(0, tasks)
    def _(o):
        d_mate(o).wait_send()

    for n in range(tasks):
        @pl.when(n != task)
        def _():
            back_copy(gi_own, gi_in, gi_ss, gi_rs, n).wait_send()
            back_copy(out_own, out_in, out_ss, out_rs, n).wait_send()


def hand_over(out_from, gi_from, gw_from, out_ref, gi_ref, gw_ref, out_here, gi_here, gw_here, in_sems, out_sems):
    members, block, _, _ = out_ref.shape
    half = block // 2
    size = gw_ref.shape[0] // 4
    moves = []
    for source, here, ref in ((gi_from, gi_here, gi_ref), (out_from, out_here, out_ref)):
        moves += [(source, here, ref, (m, pl.ds(i * half, half))) for m in range(members) for i in range(2)]
    moves += [(gw_from, gw_here, gw_ref, (pl.ds(i * size, size),)) for i in range(4)]
    loads = [pltpu.make_async_copy(a.at[w], h.at[w], in_sems.at[i]) for i, (a, h, _, w) in enumerate(moves)]
    stores = [pltpu.make_async_copy(h.at[w], r.at[w], out_sems.at[i]) for i, (_, h, r, w) in enumerate(moves)]
    for load in loads:
        load.start()
    for load, store in zip(loads, stores):
        load.wait()
        store.start()
    for store in stores:
        store.wait()


def on_device(features, weight, grad_out, band_width, band_start):
    features = jnp.transpose(features, (0, 2, 1, 3))
    grad_out = jnp.transpose(grad_out, (0, 2, 1, 3))
    members, block, rows, channels = features.shape
    count = lax.axis_size("lon")
    groups = lax.axis_size("ens")
    tasks = members * rows
    lines = groups // 2
    padded = -(-block // 16) * 16
    shard = weight.shape[0]
    piece = shard // 2
    strip_rows = piece // tasks
    vmem = pltpu.VMEM
    dma = pltpu.SemaphoreType.DMA
    field = vmem((tasks, padded, channels), BF)
    ext = vmem((count, padded, channels), BF)
    strip = vmem((K * padded, tasks * padded), BF)
    wide = vmem((K, tasks, padded, channels), BF)
    scratch = [
        vmem(features.shape, BF), vmem(features.shape, BF), field, field, ext, ext, strip, strip, strip, strip, ext, ext, wide, wide,
        vmem((groups, 2, piece, channels), BF),
        field, field, field, field,
        vmem(features.shape, BF), vmem(features.shape, BF), vmem(weight.shape, F32),
        vmem((2, 2, piece, tasks * padded), BF),
        vmem((lines, 2, piece, channels), F32),
        vmem((lines, 2, piece, channels), BF),
        vmem((lines, 2, piece, channels), BF),
        vmem((lines, 2, piece, channels), BF),
        vmem((2, piece, channels), BF),
        vmem((2, 2, piece, channels), BF),
        vmem((2, tasks, strip_rows, channels), BF),
        vmem((2, tasks, strip_rows, channels), BF),
        vmem((count, strip_rows, channels), BF),
        dma((tasks,)), dma((count,)), dma((tasks,)),
        dma((tasks,)), dma((count,)), dma((tasks,)),
        dma((2 * lines,)), dma((groups,)), dma((groups,)), dma((groups,)),
        dma((tasks,)), dma((tasks,)), dma((tasks,)), dma((tasks,)),
        dma((lines,)), dma((lines,)), dma((3, 2)), dma((2,)), dma((2, 2)),
        dma((2 * tasks,)), dma((2, tasks)), dma((tasks,)), dma((count,)), dma((tasks,)), dma((2 * members + 1,)), dma((4,)),
    ]
    scalar = pl.BlockSpec(memory_space=pltpu.SMEM)
    any_place = pl.BlockSpec(memory_space=pl.ANY)
    results = (
        jax.ShapeDtypeStruct(features.shape, BF),
        jax.ShapeDtypeStruct(features.shape, BF),
        jax.ShapeDtypeStruct(weight.shape, F32),
    )
    parts = pl.pallas_call(
        functools.partial(kernel, count, groups),
        out_shape=results,
        in_specs=[any_place, any_place, any_place, scalar, scalar],
        out_specs=(any_place,) * 3,
        scratch_shapes=scratch,
        compiler_params=pltpu.CompilerParams(
            collective_id=0, has_side_effects=True, vmem_limit_bytes=60 * 1024 * 1024
        ),
    )(features, grad_out, weight, band_width, band_start)
    output, grad_input, grad_weight = pl.pallas_call(
        hand_over,
        out_shape=results,
        in_specs=[any_place] * 3,
        out_specs=(any_place,) * 3,
        scratch_shapes=[
            vmem(features.shape, BF), vmem(features.shape, BF), vmem(weight.shape, F32),
            dma((4 * members + 4,)), dma((4 * members + 4,)),
        ],
        compiler_params=pltpu.CompilerParams(vmem_limit_bytes=60 * 1024 * 1024),
    )(*parts)
    return jnp.transpose(output, (0, 2, 1, 3)), jnp.transpose(grad_input, (0, 2, 1, 3)), grad_weight


def solution(mesh):
    placed = (P("ens", None, "lon", None), P("ens", None), P("ens", None, "lon", None), P(), P())
    return jax.shard_map(
        on_device,
        mesh=mesh,
        in_specs=placed,
        out_specs=(P("ens", None, "lon", None), P("ens", None, "lon", None), P("ens", None)),
        check_vma=False,
    )
```

```python
import functools

import jax
import jax.numpy as jnp
from jax import lax
from jax.experimental import pallas as pl
from jax.experimental.pallas import tpu as pltpu
from jax.sharding import PartitionSpec as P

K = 4
BF = jnp.bfloat16
F32 = jnp.float32


def remote(src, dst, send, recv, lon, ens):
    return pltpu.make_async_remote_copy(
        src_ref=src,
        dst_ref=dst,
        send_sem=send,
        recv_sem=recv,
        device_id={"lon": lon, "ens": ens},
        device_id_type=pl.DeviceIdType.MESH,
    )


def fill_strips(plus, minus, width, start, block, padded, count, flip):
    circle = block * count
    lanes = padded * count // 2
    step = min(128, lanes)
    row = lax.broadcasted_iota(jnp.int32, (padded, step), 0)
    lane = lax.broadcasted_iota(jnp.int32, (padded, step), 1)
    wide = jnp.full((1, step), width.astype(F32), F32)
    scale = 0.5 / jnp.sqrt(wide)
    for first in range(0, lanes, step):
        column = lane + first
        low = first // padded
        part = jnp.full_like(column, low)
        for edge in range(low + 1, (first + step - 1) // padded + 1):
            part = part + (column >= edge * padded).astype(jnp.int32)
        inner = column - part * padded
        place = inner + part * block
        valid = (inner < block) & (row < block)
        near = (row - place if flip else place - row) - start
        near = jnp.where(near < 0, near + circle, near)
        near = jnp.where(near >= circle, near - circle, near)
        far = jnp.where(near >= circle // 2, near - circle // 2, near + circle // 2)
        in_near = valid & (near < width)
        in_far = valid & (far < width)
        at_near = (near.astype(F32) + 0.5) * (K - 1) / wide
        at_far = (far.astype(F32) + 0.5) * (K - 1) / wide
        for k in range(K):
            one = jnp.where(in_near, jnp.maximum(0.0, 1.0 - jnp.abs(at_near - float(k))) * scale, 0.0)
            two = jnp.where(in_far, jnp.maximum(0.0, 1.0 - jnp.abs(at_far - float(k))) * scale, 0.0)
            where = (pl.ds(k * padded, padded), pl.ds(first, step))
            plus[where] = (one + two).astype(BF)
            minus[where] = (one - two).astype(BF)


def spread(block, padded, rows):
    to = lax.broadcasted_iota(jnp.int32, (rows * padded, block * rows), 0)
    source = lax.broadcasted_iota(jnp.int32, (rows * padded, block * rows), 1)
    row = sum((to >= padded * r).astype(jnp.int32) for r in range(1, rows))
    place = to - padded * row
    return ((source == place * rows + row) & (place < block)).astype(F32).astype(BF)


def gather_back(block, padded, rows):
    to = lax.broadcasted_iota(jnp.int32, (block * rows, rows * padded), 0)
    source = lax.broadcasted_iota(jnp.int32, (block * rows, rows * padded), 1)
    place = lax.div(to, rows)
    return (source == (to - place * rows) * padded + place).astype(F32).astype(BF)


def kernel(
    count, groups,
    f_hbm, g_hbm, w_hbm, width_ref, start_ref,
    out_ref, gi_ref, gw_ref,
    f_ref, g_ref, f_send, g_send, f_ext, g_ext, f_plus, f_minus, g_plus, g_minus, sums, differences, resp, adj, w_all,
    out_own, gi_own, out_in, gi_in, out_done, gi_done, gw_done,
    turned, gw_own, gw_half, gw_mate, gw_sum, gw_hop, gw_line, gw_cross, gw_part, gw_part_in, gw_full,
    f_ss, f_rs, f_fs, g_ss, g_rs, g_fs, w_ss, w_rs, w_ms, w_mr,
    out_ss, out_rs, gi_ss, gi_rs,
    a_ss, a_rs, b_ss, b_hs, b_rs, x_ss, x_rs, c_ss, c_rs, d_ss, d_rs, d_ms, keep_sem, load_sem,
):
    members, block, rows, channels = f_hbm.shape
    padded = f_send.shape[1]
    tasks = members * rows
    lon = lax.axis_index("lon")
    ens = lax.axis_index("ens")
    half = lax.rem(lon, 2)
    task = lax.div(lon, 2)
    mate = lon + 1 - 2 * half
    side = lax.rem(ens, 2)
    line = lax.div(ens, 2)
    lines = groups // 2
    across = ens + 1 - 2 * side
    beside = lon + 2 - 4 * lax.rem(task, 2)

    barrier = pltpu.get_barrier_semaphore()

    def greet(to_lon, to_ens):
        pl.semaphore_signal(barrier, inc=1, device_id={"lon": to_lon, "ens": to_ens}, device_id_type=pl.DeviceIdType.MESH)

    for o in range(1, tasks):
        greet(2 * lax.rem(task + o, tasks) + half, ens)
    greet(mate, ens)
    for o in range(1, lines):
        greet(lon, 2 * lax.rem(line + o, lines) + side)
    greet(beside, across)

    def stage(ref, buffer, ext):
        for m in range(members):
            flat = ref[m].reshape(block * rows, channels)
            moved = jnp.dot(to_rows, flat, preferred_element_type=F32).astype(BF)
            buffer[pl.ds(m * rows, rows)] = moved.reshape(rows, padded, channels)
        ext[lon] = buffer[task]

    piece = w_all.shape[2]
    load_g = pltpu.make_async_copy(g_hbm, g_ref, load_sem.at[0])
    load_w = [pltpu.make_async_copy(w_hbm.at[pl.ds(i * piece, piece)], w_all.at[ens, i], load_sem.at[1 + i]) for i in range(2)]
    load_f = pltpu.make_async_copy(f_hbm, f_ref, load_sem.at[3])
    for load in (load_g, *load_w, load_f):
        load.start()
    to_rows = spread(block, padded, rows)
    load_g.wait()
    stage(g_ref, g_send, g_ext)
    for load in load_w:
        load.wait()

    pl.semaphore_wait(barrier, tasks + lines)

    w_across = remote(w_all.at[ens, half], w_all.at[ens, half], w_ss.at[0], w_rs.at[ens], beside, across)

    def along(o):
        return 2 * lax.rem(line + o, lines) + side

    def w_copy(o):
        return remote(w_all.at[ens, half], w_all.at[ens, half], w_ss.at[o], w_rs.at[ens], lon, along(o))

    def w_second(o):
        return remote(w_all.at[across, half], w_all.at[across, half], w_ss.at[lines + o], w_rs.at[across], lon, along(o))

    far_first = sorted(range(1, tasks), key=lambda o: (min(o, tasks - o) < tasks // 2, o % 2 == 0, abs(o - tasks // 2)))

    def w_from(other):
        return remote(w_all.at[other, half], w_all.at[other, half], w_ss.at[0], w_rs.at[other], lon, other)

    def in_copy(buffer, ext, ss, rs, o):
        q = lax.rem(task + o, tasks)
        return remote(buffer.at[q], ext.at[lon], ss.at[o], rs.at[lon], 2 * q + half, ens)

    def in_from(ext, ss, rs, o):
        slot = 2 * lax.rem(task + tasks - o, tasks) + half
        return remote(ext.at[slot], ext.at[slot], ss.at[o], rs.at[slot], slot, ens)

    def forward(ext, fs, rs, o):
        slot = 2 * lax.rem(task + tasks - o, tasks) + half
        return remote(ext.at[slot], ext.at[slot], fs.at[o], rs.at[slot], mate, ens)

    def forwarded(ext, fs, rs, o):
        slot = 2 * lax.rem(task + tasks - o, tasks) + 1 - half
        return remote(ext.at[slot], ext.at[slot], fs.at[o], rs.at[slot], mate, ens)

    for o in far_first:
        in_copy(g_send, g_ext, g_ss, g_rs, o).start()

    w_across.start()

    @pl.loop(1, lines)
    def _(o):
        w_copy(o).start()

    forward(g_ext, g_fs, g_rs, 0).start()
    load_f.wait()
    stage(f_ref, f_send, f_ext)
    forward(f_ext, f_fs, f_rs, 0).start()

    remote(w_all.at[across, half], w_all.at[across, half], w_ss.at[0], w_rs.at[across], beside, across).wait_recv()

    @pl.loop(1, lines)
    def _(o):
        w_second(o).start()

    row = lax.rem(task, rows)
    fill_strips(g_plus, g_minus, width_ref[row], start_ref[row], block, padded, count, True)

    for o in far_first:
        in_copy(g_send, g_ext, g_ss, g_rs, o).wait_send()
        in_copy(f_send, f_ext, f_ss, f_rs, o).start()

    fill_strips(f_plus, f_minus, width_ref[row], start_ref[row], block, padded, count, False)

    def pass_on(ext, ss, fs, rs):
        for o in far_first:
            in_from(ext, ss, rs, o).wait_recv()
            forward(ext, fs, rs, o).start()

    def complete(ext, fs, rs):
        for o in (0, *far_first):
            forwarded(ext, fs, rs, o).wait_recv()

        @pl.loop(0, tasks)
        def _(b):
            one = ext[b].astype(F32)
            two = ext[tasks + b].astype(F32)
            both = (one + two).astype(BF)
            apart = one - two
            sums[b] = both
            sums[tasks + b] = both
            differences[b] = apart.astype(BF)
            differences[tasks + b] = (-apart).astype(BF)

    def convolve(plus, minus, result, which):
        @pl.loop(which * (tasks // 4), (which + 1) * (tasks // 4))
        def _(n):
            window = pl.ds(2 * n + half, tasks)
            both = jnp.dot(plus[...], sums[window].reshape(tasks * padded, channels), preferred_element_type=F32)
            apart = jnp.dot(minus[...], differences[window].reshape(tasks * padded, channels), preferred_element_type=F32)
            near = (both + apart).astype(BF)
            far = (both - apart).astype(BF)
            for k in range(K):
                result[k, n] = near[k * padded:(k + 1) * padded]
                result[k, tasks // 2 + n] = far[k * padded:(k + 1) * padded]

    def weight_of(k):
        return w_all[pl.ds(2 * k, 2)].reshape(channels, channels)

    def back_copy(own, into, ss, rs, n):
        return remote(own.at[n], into.at[task], ss.at[n], rs.at[task], 2 * n + half, ens)

    def back_from(own, into, ss, rs, n):
        return remote(own.at[n], into.at[n], ss.at[n], rs.at[n], 2 * n + half, ens)

    def mix(source, own, c, flip):
        chunk = tasks // 2
        total = None
        for k in range(K):
            part = source[k, pl.ds(c * chunk, chunk)].reshape(chunk * padded, channels)
            dims = (((1,), (1 if flip else 0,)), ((), ()))
            term = lax.dot_general(part, weight_of(k), dims, preferred_element_type=F32)
            total = term if total is None else total + term
        own[pl.ds(c * chunk, chunk)] = total.astype(BF).reshape(chunk, padded, channels)

    def send_back(own, into, ss, rs, c):
        chunk = tasks // 2
        for o in far_first:
            n = lax.rem(task + o, tasks)

            @pl.when(lax.div(n, chunk) == c)
            def _():
                back_copy(own, into, ss, rs, n).start()

    pass_on(g_ext, g_ss, g_fs, g_rs)
    complete(g_ext, g_fs, g_rs)

    def w_mate(e):
        return remote(w_all.at[e, half], w_all.at[e, half], w_ms.at[e], w_mr.at[e], mate, ens)

    def w_mate_from(e):
        return remote(w_all.at[e, 1 - half], w_all.at[e, 1 - half], w_ms.at[e], w_mr.at[e], mate, ens)

    @pl.loop(1, lines)
    def _(o):
        w_from(along(o)).wait_recv()
        w_mate(along(o)).start()

    w_mate(across).start()
    convolve(g_plus, g_minus, adj, 0)
    convolve(g_plus, g_minus, adj, 1)

    @pl.loop(1, lines)
    def _(o):
        w_from(along(o) + 1 - 2 * side).wait_recv()
        w_mate(along(o) + 1 - 2 * side).start()

    @pl.loop(1, groups)
    def _(o):
        w_mate_from(lax.rem(ens + o, groups)).wait_recv()

    first_half = 1 - lax.div(task, tasks // 2)
    for c in (first_half, 1 - first_half):
        mix(adj, gi_own, c, True)
        send_back(gi_own, gi_in, gi_ss, gi_rs, c)

    pass_on(f_ext, f_ss, f_fs, f_rs)
    own_rows = jnp.concatenate([f_ext[2 * n + half] for n in range(tasks)], axis=0)
    turned[...] = own_rows.T.reshape(turned.shape)

    def a_copy(to):
        return remote(gw_half.at[to], gw_mate.at[to], a_ss.at[to], a_rs.at[to], mate, ens)

    def terms(to, which):
        left = turned[:, which].reshape(2 * piece, tasks * padded)
        right = adj[to].reshape(tasks * padded, channels)
        return jnp.dot(left, right, preferred_element_type=F32).reshape(2, piece, channels)

    order = [lax.rem(line + o, lines) for o in (2, 1, 3, 0)]
    for to in order[:2]:
        gw_half[to] = terms(to, 1 - half).astype(BF)
        a_copy(to).start()
    gw_own[order[0]] = terms(order[0], half)

    ahead = lax.rem(line + 1, lines)
    back = lax.rem(line + lines - 1, lines)
    opposite = lax.rem(line + 2, lines)
    ways = ((0, ahead), (1, back))
    sides = (1 - side, side)
    rows_half = piece // 2

    def part(i):
        return pl.ds(i * rows_half, rows_half)

    def chip_sum(to, s, i):
        return gw_own[to, s, part(i)] + gw_mate[to, s, part(i)].astype(F32)

    def hop(t, i):
        return remote(gw_sum.at[opposite, sides[t], part(i)], gw_hop.at[t, i], b_ss.at[0, t, i], b_hs.at[t, i],
                      lon, 2 * ways[i][1] + side)

    def plain(t, i):
        return remote(gw_sum.at[ways[i][1], sides[t], part(1 - i)], gw_line.at[t, i, 1 - i], b_ss.at[1, t, i], b_rs.at[t, i, 1 - i],
                      lon, 2 * ways[i][1] + side)

    def added(t, i):
        return remote(gw_sum.at[ways[i][1], sides[t], part(i)], gw_line.at[t, i, i], b_ss.at[2, t, i], b_rs.at[t, i, i],
                      lon, 2 * ways[i][1] + side)

    def start_hop(t):
        for i in range(2):
            gw_sum[opposite, sides[t], part(i)] = chip_sum(opposite, sides[t], i).astype(BF)
            hop(t, i).start()

    def start_plain(t):
        for i, to in ways:
            gw_sum[to, sides[t], part(1 - i)] = chip_sum(to, sides[t], 1 - i).astype(BF)
            plain(t, i).start()

    def start_added(t):
        for i, to in ways:
            hop(t, i).wait_recv()
            gw_sum[to, sides[t], part(i)] = (chip_sum(to, sides[t], i) + gw_hop[t, i].astype(F32)).astype(BF)
            added(t, i).start()

    def line_sum(t):
        for i in range(2):
            plain(t, i).wait_recv()
            added(t, i).wait_recv()
        total = gw_own[line, sides[t]] + gw_mate[line, sides[t]].astype(F32)
        return total + (gw_line[t, 0].astype(F32) + gw_line[t, 1].astype(F32)).reshape(piece, channels)

    a_copy(opposite).wait_recv()
    start_hop(0)
    for to in order[2:]:
        gw_half[to] = terms(to, 1 - half).astype(BF)
        a_copy(to).start()
    for to in order[1:]:
        gw_own[to] = terms(to, half)
    for _, to in ways:
        a_copy(to).wait_recv()
    start_plain(0)
    start_hop(1)
    a_copy(line).wait_recv()

    complete(f_ext, f_fs, f_rs)
    convolve(f_plus, f_minus, resp, 0)
    start_added(0)
    start_plain(1)
    convolve(f_plus, f_minus, resp, 1)
    start_added(1)

    own_half = lax.div(task, tasks // 2)
    mix(resp, out_own, 1 - own_half, False)
    send_back(out_own, out_in, out_ss, out_rs, 1 - own_half)

    cross = remote(gw_cross.at[0], gw_cross.at[1], x_ss, x_rs, beside, across)
    gw_cross[0] = line_sum(0).astype(BF)
    cross.start()
    mix(resp, out_own, own_half, False)

    total = line_sum(1)
    cross.wait_recv()
    gw_part[...] = (total + gw_cross[1].astype(F32)).astype(BF).reshape(gw_part.shape)

    def c_copy(o):
        q = lax.rem(task + o, tasks)
        return remote(gw_part.at[q], gw_part_in.at[task], c_ss.at[o], c_rs.at[task], 2 * q + half, ens)

    def c_from(o):
        q = lax.rem(task + o, tasks)
        return remote(gw_part.at[q], gw_part_in.at[q], c_ss.at[o], c_rs.at[q], 2 * q + half, ens)

    for o in far_first:
        c_copy(o).start()

    send_back(out_own, out_in, out_ss, out_rs, own_half)
    gw_part_in[task] = gw_part[task]

    def d_copy(o):
        return remote(gw_full.at[lon], gw_full.at[lon], d_ss.at[o], d_rs.at[lon], 2 * lax.rem(task + o, tasks) + half, ens)

    def d_from(o):
        other = 2 * lax.rem(task + tasks - o, tasks) + half
        return remote(gw_full.at[other], gw_full.at[other], d_ss.at[o], d_rs.at[other], other, ens)

    def d_mate(o):
        other = 2 * lax.rem(task + tasks - o, tasks) + half
        return remote(gw_full.at[other], gw_full.at[other], d_ms.at[o], d_rs.at[other], mate, ens)

    def d_mate_from(o):
        other = 2 * lax.rem(task + tasks - o, tasks) + 1 - half
        return remote(gw_full.at[other], gw_full.at[other], d_ms.at[o], d_rs.at[other], mate, ens)

    def finish(ref, done, own, into, ss, rs, which):
        into[task] = own[task]
        keeps = []
        for m in range(members):
            for q in range(m * rows, (m + 1) * rows):
                @pl.when(q != task)
                def _():
                    back_from(own, into, ss, rs, q).wait_recv()
            flat = into[pl.ds(m * rows, rows)].reshape(rows * padded, channels)
            moved = jnp.dot(to_places, flat, preferred_element_type=F32).astype(BF)
            done[m] = moved.reshape(block, rows, channels)
            keeps.append(pltpu.make_async_copy(done.at[m], ref.at[m], keep_sem.at[which * members + m]))
            keeps[-1].start()
        return keeps

    to_places = gather_back(block, padded, rows)
    keep_gi = finish(gi_ref, gi_done, gi_own, gi_in, gi_ss, gi_rs, 0)

    for o in far_first:
        c_from(o).wait_recv()

    total = None
    for q in range(tasks):
        term = gw_part_in[q].astype(F32)
        total = term if total is None else total + term
    gw_full[lon] = total.astype(BF)

    for o in far_first:
        d_copy(o).start()

    d_mate(0).start()

    keep_out = finish(out_ref, out_done, out_own, out_in, out_ss, out_rs, 1)

    @pl.loop(1, tasks)
    def _(o):
        d_from(o).wait_recv()
        d_mate(o).start()

    @pl.loop(0, tasks)
    def _(o):
        d_mate_from(o).wait_recv()

    strip_rows = gw_full.shape[1]
    for q in range(tasks):
        for s in range(2):
            gw_done[pl.ds((s * tasks + q) * strip_rows, strip_rows), :] = gw_full[2 * q + s].astype(F32)
    keep_gw = pltpu.make_async_copy(gw_done, gw_ref, keep_sem.at[2 * members])
    keep_gw.start()
    for keep in (*keep_gi, *keep_out, keep_gw):
        keep.wait()

    w_across.wait_send()

    @pl.loop(1, lines)
    def _(o):
        w_copy(o).wait_send()
        w_second(o).wait_send()

    @pl.loop(1, groups)
    def _(o):
        w_mate(lax.rem(ens + o, groups)).wait_send()

    @pl.loop(0, lines)
    def _(o):
        a_copy(o).wait_send()

    for t in range(2):
        for i in range(2):
            hop(t, i).wait_send()
            plain(t, i).wait_send()
            added(t, i).wait_send()
    cross.wait_send()

    @pl.loop(1, tasks)
    def _(o):
        c_copy(o).wait_send()

    @pl.loop(0, tasks)
    def _(o):
        forward(g_ext, g_fs, g_rs, o).wait_send()
        forward(f_ext, f_fs, f_rs, o).wait_send()

    @pl.loop(1, tasks)
    def _(o):
        in_copy(f_send, f_ext, f_ss, f_rs, o).wait_send()

    @pl.loop(1, tasks)
    def _(o):
        d_copy(o).wait_send()

    @pl.loop(0, tasks)
    def _(o):
        d_mate(o).wait_send()

    for n in range(tasks):
        @pl.when(n != task)
        def _():
            back_copy(gi_own, gi_in, gi_ss, gi_rs, n).wait_send()
            back_copy(out_own, out_in, out_ss, out_rs, n).wait_send()


def hand_over(out_from, gi_from, gw_from, out_ref, gi_ref, gw_ref, out_here, gi_here, gw_here, in_sems, out_sems):
    members, block, _, _ = out_ref.shape
    half = block // 2
    size = gw_ref.shape[0] // 4
    moves = []
    for source, here, ref in ((gi_from, gi_here, gi_ref), (out_from, out_here, out_ref)):
        moves += [(source, here, ref, (m, pl.ds(i * half, half))) for m in range(members) for i in range(2)]
    moves += [(gw_from, gw_here, gw_ref, (pl.ds(i * size, size),)) for i in range(4)]
    loads = [pltpu.make_async_copy(a.at[w], h.at[w], in_sems.at[i]) for i, (a, h, _, w) in enumerate(moves)]
    stores = [pltpu.make_async_copy(h.at[w], r.at[w], out_sems.at[i]) for i, (_, h, r, w) in enumerate(moves)]
    for load in loads:
        load.start()
    for load, store in zip(loads, stores):
        load.wait()
        store.start()
    for store in stores:
        store.wait()


def on_device(features, weight, grad_out, band_width, band_start):
    features = jnp.transpose(features, (0, 2, 1, 3))
    grad_out = jnp.transpose(grad_out, (0, 2, 1, 3))
    members, block, rows, channels = features.shape
    count = lax.axis_size("lon")
    groups = lax.axis_size("ens")
    tasks = members * rows
    lines = groups // 2
    padded = -(-block // 16) * 16
    shard = weight.shape[0]
    piece = shard // 2
    strip_rows = piece // tasks
    vmem = pltpu.VMEM
    dma = pltpu.SemaphoreType.DMA
    field = vmem((tasks, padded, channels), BF)
    ext = vmem((count, padded, channels), BF)
    strip = vmem((K * padded, tasks * padded), BF)
    wide = vmem((K, tasks, padded, channels), BF)
    scratch = [
        vmem(features.shape, BF), vmem(features.shape, BF), field, field, ext, ext, strip, strip, strip, strip, ext, ext, wide, wide,
        vmem((groups, 2, piece, channels), BF),
        field, field, field, field,
        vmem(features.shape, BF), vmem(features.shape, BF), vmem(weight.shape, F32),
        vmem((2, 2, piece, tasks * padded), BF),
        vmem((lines, 2, piece, channels), F32),
        vmem((lines, 2, piece, channels), BF),
        vmem((lines, 2, piece, channels), BF),
        vmem((lines, 2, piece, channels), BF),
        vmem((2, 2, piece // 2, channels), BF),
        vmem((2, 2, 2, piece // 2, channels), BF),
        vmem((2, piece, channels), BF),
        vmem((tasks, strip_rows, channels), BF),
        vmem((tasks, strip_rows, channels), BF),
        vmem((count, strip_rows, channels), BF),
        dma((tasks,)), dma((count,)), dma((tasks,)),
        dma((tasks,)), dma((count,)), dma((tasks,)),
        dma((2 * lines,)), dma((groups,)), dma((groups,)), dma((groups,)),
        dma((tasks,)), dma((tasks,)), dma((tasks,)), dma((tasks,)),
        dma((lines,)), dma((lines,)), dma((3, 2, 2)), dma((2, 2)), dma((2, 2, 2)), dma(()), dma(()),
        dma((tasks,)), dma((tasks,)), dma((tasks,)), dma((count,)), dma((tasks,)), dma((2 * members + 1,)), dma((4,)),
    ]
    scalar = pl.BlockSpec(memory_space=pltpu.SMEM)
    any_place = pl.BlockSpec(memory_space=pl.ANY)
    results = (
        jax.ShapeDtypeStruct(features.shape, BF),
        jax.ShapeDtypeStruct(features.shape, BF),
        jax.ShapeDtypeStruct(weight.shape, F32),
    )
    parts = pl.pallas_call(
        functools.partial(kernel, count, groups),
        out_shape=results,
        in_specs=[any_place, any_place, any_place, scalar, scalar],
        out_specs=(any_place,) * 3,
        scratch_shapes=scratch,
        compiler_params=pltpu.CompilerParams(
            collective_id=0, has_side_effects=True, vmem_limit_bytes=60 * 1024 * 1024
        ),
    )(features, grad_out, weight, band_width, band_start)
    output, grad_input, grad_weight = pl.pallas_call(
        hand_over,
        out_shape=results,
        in_specs=[any_place] * 3,
        out_specs=(any_place,) * 3,
        scratch_shapes=[
            vmem(features.shape, BF), vmem(features.shape, BF), vmem(weight.shape, F32),
            dma((4 * members + 4,)), dma((4 * members + 4,)),
        ],
        compiler_params=pltpu.CompilerParams(vmem_limit_bytes=60 * 1024 * 1024),
    )(*parts)
    return jnp.transpose(output, (0, 2, 1, 3)), jnp.transpose(grad_input, (0, 2, 1, 3)), grad_weight


def solution(mesh):
    placed = (P("ens", None, "lon", None), P("ens", None), P("ens", None, "lon", None), P(), P())
    return jax.shard_map(
        on_device,
        mesh=mesh,
        in_specs=placed,
        out_specs=(P("ens", None, "lon", None), P("ens", None, "lon", None), P("ens", None)),
        check_vma=False,
    )
```

```python
import functools

import jax
import jax.numpy as jnp
from jax import lax
from jax.experimental import pallas as pl
from jax.experimental.pallas import tpu as pltpu
from jax.sharding import PartitionSpec as P

K = 4
BF = jnp.bfloat16
F32 = jnp.float32


def remote(src, dst, send, recv, lon, ens):
    return pltpu.make_async_remote_copy(
        src_ref=src,
        dst_ref=dst,
        send_sem=send,
        recv_sem=recv,
        device_id={"lon": lon, "ens": ens},
        device_id_type=pl.DeviceIdType.MESH,
    )


def fill_strips(plus, minus, width, start, block, padded, count, flip):
    circle = block * count
    lanes = padded * count // 2
    step = min(128, lanes)
    row = lax.broadcasted_iota(jnp.int32, (padded, step), 0)
    lane = lax.broadcasted_iota(jnp.int32, (padded, step), 1)
    wide = jnp.full((1, step), width.astype(F32), F32)
    scale = 0.5 / jnp.sqrt(wide)
    for first in range(0, lanes, step):
        column = lane + first
        low = first // padded
        part = jnp.full_like(column, low)
        for edge in range(low + 1, (first + step - 1) // padded + 1):
            part = part + (column >= edge * padded).astype(jnp.int32)
        inner = column - part * padded
        place = inner + part * block
        valid = (inner < block) & (row < block)
        near = (row - place if flip else place - row) - start
        near = jnp.where(near < 0, near + circle, near)
        near = jnp.where(near >= circle, near - circle, near)
        far = jnp.where(near >= circle // 2, near - circle // 2, near + circle // 2)
        in_near = valid & (near < width)
        in_far = valid & (far < width)
        at_near = (near.astype(F32) + 0.5) * (K - 1) / wide
        at_far = (far.astype(F32) + 0.5) * (K - 1) / wide
        for k in range(K):
            one = jnp.where(in_near, jnp.maximum(0.0, 1.0 - jnp.abs(at_near - float(k))) * scale, 0.0)
            two = jnp.where(in_far, jnp.maximum(0.0, 1.0 - jnp.abs(at_far - float(k))) * scale, 0.0)
            where = (pl.ds(k * padded, padded), pl.ds(first, step))
            plus[where] = (one + two).astype(BF)
            minus[where] = (one - two).astype(BF)


def spread(block, padded, rows):
    to = lax.broadcasted_iota(jnp.int32, (rows * padded, block * rows), 0)
    source = lax.broadcasted_iota(jnp.int32, (rows * padded, block * rows), 1)
    row = sum((to >= padded * r).astype(jnp.int32) for r in range(1, rows))
    place = to - padded * row
    return ((source == place * rows + row) & (place < block)).astype(F32).astype(BF)


def gather_back(block, padded, rows):
    to = lax.broadcasted_iota(jnp.int32, (block * rows, rows * padded), 0)
    source = lax.broadcasted_iota(jnp.int32, (block * rows, rows * padded), 1)
    place = lax.div(to, rows)
    return (source == (to - place * rows) * padded + place).astype(F32).astype(BF)


def kernel(
    count, groups,
    f_hbm, g_hbm, w_hbm, width_ref, start_ref,
    out_ref, gi_ref, gw_ref,
    f_ref, g_ref, f_send, g_send, f_ext, g_ext, f_plus, f_minus, g_plus, g_minus, sums, differences, resp, adj, w_all,
    out_own, gi_own, out_in, gi_in, out_done, gi_done, gw_done,
    turned, gw_own, gw_half, gw_mate, gw_sum, gw_hop, gw_line, gw_cross, gw_part, gw_part_in, gw_full,
    f_ss, f_rs, f_fs, g_ss, g_rs, g_fs, w_ss, w_rs, w_ms, w_mr,
    out_ss, out_rs, gi_ss, gi_rs,
    a_ss, a_rs, b_ss, b_hs, b_rs, x_ss, x_rs, c_ss, c_rs, d_ss, d_rs, d_ms, keep_sem, load_sem,
):
    members, block, rows, channels = f_hbm.shape
    padded = f_send.shape[1]
    tasks = members * rows
    lon = lax.axis_index("lon")
    ens = lax.axis_index("ens")
    half = lax.rem(lon, 2)
    task = lax.div(lon, 2)
    mate = lon + 1 - 2 * half
    side = lax.rem(ens, 2)
    line = lax.div(ens, 2)
    lines = groups // 2
    across = ens + 1 - 2 * side
    beside = lon + 2 - 4 * lax.rem(task, 2)

    barrier = pltpu.get_barrier_semaphore()

    def greet(to_lon, to_ens):
        pl.semaphore_signal(barrier, inc=1, device_id={"lon": to_lon, "ens": to_ens}, device_id_type=pl.DeviceIdType.MESH)

    for o in range(1, tasks):
        greet(2 * lax.rem(task + o, tasks) + half, ens)
    greet(mate, ens)
    for o in range(1, lines):
        greet(lon, 2 * lax.rem(line + o, lines) + side)
    greet(beside, across)

    def stage_member(ref, buffer, m):
        flat = ref[m].reshape(block * rows, channels)
        moved = jnp.dot(to_rows, flat, preferred_element_type=F32).astype(BF)
        buffer[pl.ds(m * rows, rows)] = moved.reshape(rows, padded, channels)

    def stage(ref, buffer, ext):
        for m in range(members):
            stage_member(ref, buffer, m)
        ext[lon] = buffer[task]

    piece = w_all.shape[2]
    load_g = [pltpu.make_async_copy(g_hbm.at[m], g_ref.at[m], load_sem.at[4 + m]) for m in range(members)]
    load_w = [pltpu.make_async_copy(w_hbm.at[pl.ds(i * piece, piece)], w_all.at[ens, i], load_sem.at[1 + i]) for i in range(2)]
    load_f = pltpu.make_async_copy(f_hbm, f_ref, load_sem.at[3])
    for load in (*load_g, *load_w, load_f):
        load.start()
    to_rows = spread(block, padded, rows)
    load_g[0].wait()
    stage_member(g_ref, g_send, 0)

    pl.semaphore_wait(barrier, tasks + lines)

    w_across = remote(w_all.at[ens, half], w_all.at[ens, half], w_ss.at[0], w_rs.at[ens], beside, across)

    def along(o):
        return 2 * lax.rem(line + o, lines) + side

    def w_copy(o):
        return remote(w_all.at[ens, half], w_all.at[ens, half], w_ss.at[o], w_rs.at[ens], lon, along(o))

    def w_second(o):
        return remote(w_all.at[across, half], w_all.at[across, half], w_ss.at[lines + o], w_rs.at[across], lon, along(o))

    far_first = sorted(range(1, tasks), key=lambda o: (min(o, tasks - o) < tasks // 2, o % 2 == 0, abs(o - tasks // 2)))

    def w_from(other):
        return remote(w_all.at[other, half], w_all.at[other, half], w_ss.at[0], w_rs.at[other], lon, other)

    def in_copy(buffer, ext, ss, rs, o):
        q = lax.rem(task + o, tasks)
        return remote(buffer.at[q], ext.at[lon], ss.at[o], rs.at[lon], 2 * q + half, ens)

    def in_from(ext, ss, rs, o):
        slot = 2 * lax.rem(task + tasks - o, tasks) + half
        return remote(ext.at[slot], ext.at[slot], ss.at[o], rs.at[slot], slot, ens)

    def forward(ext, fs, rs, o):
        slot = 2 * lax.rem(task + tasks - o, tasks) + half
        return remote(ext.at[slot], ext.at[slot], fs.at[o], rs.at[slot], mate, ens)

    def forwarded(ext, fs, rs, o):
        slot = 2 * lax.rem(task + tasks - o, tasks) + 1 - half
        return remote(ext.at[slot], ext.at[slot], fs.at[o], rs.at[slot], mate, ens)

    for m in range(members):
        if m:
            load_g[m].wait()
            stage_member(g_ref, g_send, m)
        for o in far_first:
            @pl.when(lax.div(lax.rem(task + o, tasks), rows) == m)
            def _():
                in_copy(g_send, g_ext, g_ss, g_rs, o).start()
    g_ext[lon] = g_send[task]
    for load in load_w:
        load.wait()

    w_across.start()

    @pl.loop(1, lines)
    def _(o):
        w_copy(o).start()

    forward(g_ext, g_fs, g_rs, 0).start()
    load_f.wait()
    stage(f_ref, f_send, f_ext)
    forward(f_ext, f_fs, f_rs, 0).start()

    remote(w_all.at[across, half], w_all.at[across, half], w_ss.at[0], w_rs.at[across], beside, across).wait_recv()

    @pl.loop(1, lines)
    def _(o):
        w_second(o).start()

    row = lax.rem(task, rows)
    fill_strips(g_plus, g_minus, width_ref[row], start_ref[row], block, padded, count, True)

    for o in far_first:
        in_copy(g_send, g_ext, g_ss, g_rs, o).wait_send()
        in_copy(f_send, f_ext, f_ss, f_rs, o).start()

    fill_strips(f_plus, f_minus, width_ref[row], start_ref[row], block, padded, count, False)

    def pass_on(ext, ss, fs, rs):
        for o in far_first:
            in_from(ext, ss, rs, o).wait_recv()
            forward(ext, fs, rs, o).start()

    def complete(ext, fs, rs):
        for o in (0, *far_first):
            forwarded(ext, fs, rs, o).wait_recv()

        @pl.loop(0, tasks)
        def _(b):
            one = ext[b].astype(F32)
            two = ext[tasks + b].astype(F32)
            both = (one + two).astype(BF)
            apart = one - two
            sums[b] = both
            sums[tasks + b] = both
            differences[b] = apart.astype(BF)
            differences[tasks + b] = (-apart).astype(BF)

    def convolve(plus, minus, result, which):
        @pl.loop(which * (tasks // 4), (which + 1) * (tasks // 4))
        def _(n):
            window = pl.ds(2 * n + half, tasks)
            both = jnp.dot(plus[...], sums[window].reshape(tasks * padded, channels), preferred_element_type=F32)
            apart = jnp.dot(minus[...], differences[window].reshape(tasks * padded, channels), preferred_element_type=F32)
            near = (both + apart).astype(BF)
            far = (both - apart).astype(BF)
            for k in range(K):
                result[k, n] = near[k * padded:(k + 1) * padded]
                result[k, tasks // 2 + n] = far[k * padded:(k + 1) * padded]

    def weight_of(k):
        return w_all[pl.ds(2 * k, 2)].reshape(channels, channels)

    def back_copy(own, into, ss, rs, n):
        return remote(own.at[n], into.at[task], ss.at[n], rs.at[task], 2 * n + half, ens)

    def back_from(own, into, ss, rs, n):
        return remote(own.at[n], into.at[n], ss.at[n], rs.at[n], 2 * n + half, ens)

    def mix(source, own, c, flip):
        chunk = tasks // 2
        total = None
        for k in range(K):
            part = source[k, pl.ds(c * chunk, chunk)].reshape(chunk * padded, channels)
            dims = (((1,), (1 if flip else 0,)), ((), ()))
            term = lax.dot_general(part, weight_of(k), dims, preferred_element_type=F32)
            total = term if total is None else total + term
        own[pl.ds(c * chunk, chunk)] = total.astype(BF).reshape(chunk, padded, channels)

    def send_back(own, into, ss, rs, c):
        chunk = tasks // 2
        for o in far_first:
            n = lax.rem(task + o, tasks)

            @pl.when(lax.div(n, chunk) == c)
            def _():
                back_copy(own, into, ss, rs, n).start()

    pass_on(g_ext, g_ss, g_fs, g_rs)
    complete(g_ext, g_fs, g_rs)

    def w_mate(e):
        return remote(w_all.at[e, half], w_all.at[e, half], w_ms.at[e], w_mr.at[e], mate, ens)

    def w_mate_from(e):
        return remote(w_all.at[e, 1 - half], w_all.at[e, 1 - half], w_ms.at[e], w_mr.at[e], mate, ens)

    @pl.loop(1, lines)
    def _(o):
        w_from(along(o)).wait_recv()
        w_mate(along(o)).start()

    w_mate(across).start()
    convolve(g_plus, g_minus, adj, 0)
    convolve(g_plus, g_minus, adj, 1)

    @pl.loop(1, lines)
    def _(o):
        w_from(along(o) + 1 - 2 * side).wait_recv()
        w_mate(along(o) + 1 - 2 * side).start()

    @pl.loop(1, groups)
    def _(o):
        w_mate_from(lax.rem(ens + o, groups)).wait_recv()

    first_half = 1 - lax.div(task, tasks // 2)
    for c in (first_half, 1 - first_half):
        mix(adj, gi_own, c, True)
        send_back(gi_own, gi_in, gi_ss, gi_rs, c)

    pass_on(f_ext, f_ss, f_fs, f_rs)
    own_rows = jnp.concatenate([f_ext[2 * n + half] for n in range(tasks)], axis=0)
    turned[...] = own_rows.T.reshape(turned.shape)

    def a_copy(to):
        return remote(gw_half.at[to], gw_mate.at[to], a_ss.at[to], a_rs.at[to], mate, ens)

    def terms(to, which):
        left = turned[:, which].reshape(2 * piece, tasks * padded)
        right = adj[to].reshape(tasks * padded, channels)
        return jnp.dot(left, right, preferred_element_type=F32).reshape(2, piece, channels)

    order = [lax.rem(line + o, lines) for o in (2, 1, 3, 0)]
    for to in order[:2]:
        gw_half[to] = terms(to, 1 - half).astype(BF)
        a_copy(to).start()
    gw_own[order[0]] = terms(order[0], half)

    ahead = lax.rem(line + 1, lines)
    back = lax.rem(line + lines - 1, lines)
    opposite = lax.rem(line + 2, lines)
    ways = ((0, ahead), (1, back))
    sides = (1 - side, side)
    rows_half = piece // 2

    def part(i):
        return pl.ds(i * rows_half, rows_half)

    def chip_sum(to, s, i):
        return gw_own[to, s, part(i)] + gw_mate[to, s, part(i)].astype(F32)

    def hop(t, i):
        return remote(gw_sum.at[opposite, sides[t], part(i)], gw_hop.at[t, i], b_ss.at[0, t, i], b_hs.at[t, i],
                      lon, 2 * ways[i][1] + side)

    def plain(t, i):
        return remote(gw_sum.at[ways[i][1], sides[t], part(1 - i)], gw_line.at[t, i, 1 - i], b_ss.at[1, t, i], b_rs.at[t, i, 1 - i],
                      lon, 2 * ways[i][1] + side)

    def added(t, i):
        return remote(gw_sum.at[ways[i][1], sides[t], part(i)], gw_line.at[t, i, i], b_ss.at[2, t, i], b_rs.at[t, i, i],
                      lon, 2 * ways[i][1] + side)

    def start_hop(t):
        for i in range(2):
            gw_sum[opposite, sides[t], part(i)] = chip_sum(opposite, sides[t], i).astype(BF)
            hop(t, i).start()

    def start_plain(t):
        for i, to in ways:
            gw_sum[to, sides[t], part(1 - i)] = chip_sum(to, sides[t], 1 - i).astype(BF)
            plain(t, i).start()

    def start_added(t):
        for i, to in ways:
            hop(t, i).wait_recv()
            gw_sum[to, sides[t], part(i)] = (chip_sum(to, sides[t], i) + gw_hop[t, i].astype(F32)).astype(BF)
            added(t, i).start()

    def line_sum(t):
        for i in range(2):
            plain(t, i).wait_recv()
            added(t, i).wait_recv()
        total = gw_own[line, sides[t]] + gw_mate[line, sides[t]].astype(F32)
        return total + (gw_line[t, 0].astype(F32) + gw_line[t, 1].astype(F32)).reshape(piece, channels)

    a_copy(opposite).wait_recv()
    start_hop(0)
    for to in order[2:]:
        gw_half[to] = terms(to, 1 - half).astype(BF)
        a_copy(to).start()
    for to in order[1:]:
        gw_own[to] = terms(to, half)
    for _, to in ways:
        a_copy(to).wait_recv()
    start_plain(0)
    start_hop(1)
    a_copy(line).wait_recv()

    complete(f_ext, f_fs, f_rs)
    convolve(f_plus, f_minus, resp, 0)
    start_added(0)
    start_plain(1)
    convolve(f_plus, f_minus, resp, 1)
    start_added(1)

    own_half = lax.div(task, tasks // 2)
    mix(resp, out_own, 1 - own_half, False)
    send_back(out_own, out_in, out_ss, out_rs, 1 - own_half)

    cross = remote(gw_cross.at[0], gw_cross.at[1], x_ss, x_rs, beside, across)
    gw_cross[0] = line_sum(0).astype(BF)
    cross.start()
    mix(resp, out_own, own_half, False)

    total = line_sum(1)
    cross.wait_recv()
    gw_part[...] = (total + gw_cross[1].astype(F32)).astype(BF).reshape(gw_part.shape)

    def c_copy(o):
        q = lax.rem(task + o, tasks)
        return remote(gw_part.at[q], gw_part_in.at[task], c_ss.at[o], c_rs.at[task], 2 * q + half, ens)

    def c_from(o):
        q = lax.rem(task + o, tasks)
        return remote(gw_part.at[q], gw_part_in.at[q], c_ss.at[o], c_rs.at[q], 2 * q + half, ens)

    for o in far_first:
        c_copy(o).start()

    send_back(out_own, out_in, out_ss, out_rs, own_half)
    gw_part_in[task] = gw_part[task]

    def d_copy(o):
        return remote(gw_full.at[lon], gw_full.at[lon], d_ss.at[o], d_rs.at[lon], 2 * lax.rem(task + o, tasks) + half, ens)

    def d_from(o):
        other = 2 * lax.rem(task + tasks - o, tasks) + half
        return remote(gw_full.at[other], gw_full.at[other], d_ss.at[o], d_rs.at[other], other, ens)

    def d_mate(o):
        other = 2 * lax.rem(task + tasks - o, tasks) + half
        return remote(gw_full.at[other], gw_full.at[other], d_ms.at[o], d_rs.at[other], mate, ens)

    def d_mate_from(o):
        other = 2 * lax.rem(task + tasks - o, tasks) + 1 - half
        return remote(gw_full.at[other], gw_full.at[other], d_ms.at[o], d_rs.at[other], mate, ens)

    def finish(ref, done, own, into, ss, rs, which):
        into[task] = own[task]
        keeps = []
        for m in range(members):
            for q in range(m * rows, (m + 1) * rows):
                @pl.when(q != task)
                def _():
                    back_from(own, into, ss, rs, q).wait_recv()
            flat = into[pl.ds(m * rows, rows)].reshape(rows * padded, channels)
            moved = jnp.dot(to_places, flat, preferred_element_type=F32).astype(BF)
            done[m] = moved.reshape(block, rows, channels)
            keeps.append(pltpu.make_async_copy(done.at[m], ref.at[m], keep_sem.at[which * members + m]))
            keeps[-1].start()
        return keeps

    to_places = gather_back(block, padded, rows)
    keep_gi = finish(gi_ref, gi_done, gi_own, gi_in, gi_ss, gi_rs, 0)

    for o in far_first:
        c_from(o).wait_recv()

    total = None
    for q in range(tasks):
        term = gw_part_in[q].astype(F32)
        total = term if total is None else total + term
    gw_full[lon] = total.astype(BF)

    for o in far_first:
        d_copy(o).start()

    d_mate(0).start()

    keep_out = finish(out_ref, out_done, out_own, out_in, out_ss, out_rs, 1)

    @pl.loop(1, tasks)
    def _(o):
        d_from(o).wait_recv()
        d_mate(o).start()

    @pl.loop(0, tasks)
    def _(o):
        d_mate_from(o).wait_recv()

    strip_rows = gw_full.shape[1]
    for q in range(tasks):
        for s in range(2):
            gw_done[pl.ds((s * tasks + q) * strip_rows, strip_rows), :] = gw_full[2 * q + s].astype(F32)
    keep_gw = pltpu.make_async_copy(gw_done, gw_ref, keep_sem.at[2 * members])
    keep_gw.start()
    for keep in (*keep_gi, *keep_out, keep_gw):
        keep.wait()

    w_across.wait_send()

    @pl.loop(1, lines)
    def _(o):
        w_copy(o).wait_send()
        w_second(o).wait_send()

    @pl.loop(1, groups)
    def _(o):
        w_mate(lax.rem(ens + o, groups)).wait_send()

    @pl.loop(0, lines)
    def _(o):
        a_copy(o).wait_send()

    for t in range(2):
        for i in range(2):
            hop(t, i).wait_send()
            plain(t, i).wait_send()
            added(t, i).wait_send()
    cross.wait_send()

    @pl.loop(1, tasks)
    def _(o):
        c_copy(o).wait_send()

    @pl.loop(0, tasks)
    def _(o):
        forward(g_ext, g_fs, g_rs, o).wait_send()
        forward(f_ext, f_fs, f_rs, o).wait_send()

    @pl.loop(1, tasks)
    def _(o):
        in_copy(f_send, f_ext, f_ss, f_rs, o).wait_send()

    @pl.loop(1, tasks)
    def _(o):
        d_copy(o).wait_send()

    @pl.loop(0, tasks)
    def _(o):
        d_mate(o).wait_send()

    for n in range(tasks):
        @pl.when(n != task)
        def _():
            back_copy(gi_own, gi_in, gi_ss, gi_rs, n).wait_send()
            back_copy(out_own, out_in, out_ss, out_rs, n).wait_send()


def hand_over(out_from, gi_from, gw_from, out_ref, gi_ref, gw_ref, out_here, gi_here, gw_here, in_sems, out_sems):
    members, block, _, _ = out_ref.shape
    half = block // 2
    size = gw_ref.shape[0] // 4
    moves = []
    for source, here, ref in ((gi_from, gi_here, gi_ref), (out_from, out_here, out_ref)):
        moves += [(source, here, ref, (m, pl.ds(i * half, half))) for m in range(members) for i in range(2)]
    moves += [(gw_from, gw_here, gw_ref, (pl.ds(i * size, size),)) for i in range(4)]
    loads = [pltpu.make_async_copy(a.at[w], h.at[w], in_sems.at[i]) for i, (a, h, _, w) in enumerate(moves)]
    stores = [pltpu.make_async_copy(h.at[w], r.at[w], out_sems.at[i]) for i, (_, h, r, w) in enumerate(moves)]
    for load in loads:
        load.start()
    for load, store in zip(loads, stores):
        load.wait()
        store.start()
    for store in stores:
        store.wait()


def on_device(features, weight, grad_out, band_width, band_start):
    features = jnp.transpose(features, (0, 2, 1, 3))
    grad_out = jnp.transpose(grad_out, (0, 2, 1, 3))
    members, block, rows, channels = features.shape
    count = lax.axis_size("lon")
    groups = lax.axis_size("ens")
    tasks = members * rows
    lines = groups // 2
    padded = -(-block // 16) * 16
    shard = weight.shape[0]
    piece = shard // 2
    strip_rows = piece // tasks
    vmem = pltpu.VMEM
    dma = pltpu.SemaphoreType.DMA
    field = vmem((tasks, padded, channels), BF)
    ext = vmem((count, padded, channels), BF)
    strip = vmem((K * padded, tasks * padded), BF)
    wide = vmem((K, tasks, padded, channels), BF)
    scratch = [
        vmem(features.shape, BF), vmem(features.shape, BF), field, field, ext, ext, strip, strip, strip, strip, ext, ext, wide, wide,
        vmem((groups, 2, piece, channels), BF),
        field, field, field, field,
        vmem(features.shape, BF), vmem(features.shape, BF), vmem(weight.shape, F32),
        vmem((2, 2, piece, tasks * padded), BF),
        vmem((lines, 2, piece, channels), F32),
        vmem((lines, 2, piece, channels), BF),
        vmem((lines, 2, piece, channels), BF),
        vmem((lines, 2, piece, channels), BF),
        vmem((2, 2, piece // 2, channels), BF),
        vmem((2, 2, 2, piece // 2, channels), BF),
        vmem((2, piece, channels), BF),
        vmem((tasks, strip_rows, channels), BF),
        vmem((tasks, strip_rows, channels), BF),
        vmem((count, strip_rows, channels), BF),
        dma((tasks,)), dma((count,)), dma((tasks,)),
        dma((tasks,)), dma((count,)), dma((tasks,)),
        dma((2 * lines,)), dma((groups,)), dma((groups,)), dma((groups,)),
        dma((tasks,)), dma((tasks,)), dma((tasks,)), dma((tasks,)),
        dma((lines,)), dma((lines,)), dma((3, 2, 2)), dma((2, 2)), dma((2, 2, 2)), dma(()), dma(()),
        dma((tasks,)), dma((tasks,)), dma((tasks,)), dma((count,)), dma((tasks,)), dma((2 * members + 1,)), dma((4 + members,)),
    ]
    scalar = pl.BlockSpec(memory_space=pltpu.SMEM)
    any_place = pl.BlockSpec(memory_space=pl.ANY)
    results = (
        jax.ShapeDtypeStruct(features.shape, BF),
        jax.ShapeDtypeStruct(features.shape, BF),
        jax.ShapeDtypeStruct(weight.shape, F32),
    )
    parts = pl.pallas_call(
        functools.partial(kernel, count, groups),
        out_shape=results,
        in_specs=[any_place, any_place, any_place, scalar, scalar],
        out_specs=(any_place,) * 3,
        scratch_shapes=scratch,
        compiler_params=pltpu.CompilerParams(
            collective_id=0, has_side_effects=True, vmem_limit_bytes=60 * 1024 * 1024
        ),
    )(features, grad_out, weight, band_width, band_start)
    output, grad_input, grad_weight = pl.pallas_call(
        hand_over,
        out_shape=results,
        in_specs=[any_place] * 3,
        out_specs=(any_place,) * 3,
        scratch_shapes=[
            vmem(features.shape, BF), vmem(features.shape, BF), vmem(weight.shape, F32),
            dma((4 * members + 4,)), dma((4 * members + 4,)),
        ],
        compiler_params=pltpu.CompilerParams(vmem_limit_bytes=60 * 1024 * 1024),
    )(*parts)
    return jnp.transpose(output, (0, 2, 1, 3)), jnp.transpose(grad_input, (0, 2, 1, 3)), grad_weight


def solution(mesh):
    placed = (P("ens", None, "lon", None), P("ens", None), P("ens", None, "lon", None), P(), P())
    return jax.shard_map(
        on_device,
        mesh=mesh,
        in_specs=placed,
        out_specs=(P("ens", None, "lon", None), P("ens", None, "lon", None), P("ens", None)),
        check_vma=False,
    )
```
